32 devices in a mesh: rows: 32 (over z, y, x, core).
Axes of the slice: x: 2, y: 2, z: 4, core: 2. Of those that a mesh axis runs over, the one named last changes fastest.
Arguments:
- points_t: float32 [64, 32768], P(None, 'rows'), may hold values from -6 to 6
- pivots: int32 [2, 256], replicated, may hold values from 0 to 32767, as said below
Outputs:
- factor: bfloat16 [32768, 512], P('rows')
- residual_diag: float32 [32768], P('rows')
The draws below stay inside these ranges and needn't reach their ends.
Inputs may be any that keep to these rules, and one draw needn't show every extreme that they name: `pivots`: all 512 indices are different. In each block at most 10 indices fall in one device's points, rows k * 1024 to (k + 1) * 1024 - 1, and in each block some device holds exactly 10.
All inputs are finite; a program needn't handle non-finite values.
Results may differ from the reference program's by a relative error of at most 0.001.
Values sent between devices are 32-bit elements; how exact they have to be, the bound alone decides.
No kernel may reach another device: no remote copies, remote signals or barrier semaphores. Data moves between devices by JAX's collectives and lax.ppermute only.
A program may use at most 64 MiB of HBM per device.

```python
import jax
import jax.numpy as jnp
from jax import lax

DIM = 64
PIV = 256
BLOCKS = 2
PTS_DEV = 1024
POINTS = 32768
CAP = 10


def draw_pivots(key, part):
    ndev = POINTS // PTS_DEV
    span = PTS_DEV // (3 * CAP)
    result = []
    for block in range(BLOCKS):
        kblock = jax.random.fold_in(key, 17 + block)
        kperm = jax.random.fold_in(kblock, 1)
        koff = jax.random.fold_in(kblock, 2)
        kshuf = jax.random.fold_in(kblock, 3)
        slots = jax.random.permutation(kperm, ndev * CAP).astype(jnp.int32)
        busiest = slots[0] // CAP
        full = busiest * CAP + jnp.arange(CAP, dtype=jnp.int32)
        owners = slots // CAP
        order_key = jnp.where(owners == busiest, ndev * CAP + jnp.arange(ndev * CAP, dtype=jnp.int32), jnp.arange(ndev * CAP, dtype=jnp.int32))
        order = jnp.argsort(order_key, stable=True)
        rest = slots[order][:PIV - CAP]
        chosen = jnp.concatenate([full, rest])
        owner = chosen // CAP
        sub = chosen % CAP
        offset = jax.random.randint(koff, (PIV,), 0, span).astype(jnp.int32)
        local = (block * CAP + sub) * span + offset
        index = owner * PTS_DEV + local
        shuffle = jax.random.permutation(kshuf, PIV)
        result.append(index[shuffle])
    return jnp.stack(result).astype(jnp.int32)


def steps_of(rng, extent, split, least, high):
    def one(axis_at, shards_of):
        draws = jax.random.uniform(jax.random.fold_in(jax.random.fold_in(rng, 6), axis_at), (shards_of,), jnp.float32, least / len(split), high / len(split))
        return jnp.repeat(jnp.exp(draws), extent[axis_at] // shards_of).reshape((-1,) + (1,) * (len(extent) - axis_at - 1))

    loudness = one(*split[0])
    for cut in split[1:]:
        loudness = loudness * one(*cut)
    return loudness


def scatter_about(rng, extent, spread, limit, pieces=(), held_as=jnp.bfloat16):
    entries = jax.random.normal(rng, extent, jnp.float32) * spread
    if len(pieces) > 0:
        entries = steps_of(rng, extent, pieces, -0.22, 0.18) * entries
    return jnp.clip(entries, min=-limit, max=limit).astype(held_as)


def setup_inputs(seed: int = 0) -> dict:
    keys = jax.random.split(jax.random.key(seed), 3)
    return {
        "points_t": scatter_about(keys[0], (DIM, POINTS), 1.0, 6.0, ((1, 32),), jnp.float32),
        "pivots": draw_pivots(jax.random.fold_in(keys[2], 71), 0),
    }


def kernel(left_t, right_t):
    cross = lax.dot_general(left_t.astype(jnp.float32), right_t.astype(jnp.float32), (((0,), (0,)), ((), ())), precision=lax.Precision.HIGHEST, preferred_element_type=jnp.float32)
    sq = jnp.sum(left_t * left_t, 0)[:, None] + jnp.sum(right_t * right_t, 0)[None, :] - 2.0 * cross
    return jnp.exp(-sq / (1.65 * DIM))

def reference(points_t, pivots):
    nblocks = POINTS // PTS_DEV
    point_blocks = points_t.reshape(DIM, nblocks, PTS_DEV).transpose(1, 0, 2)
    factor = jnp.zeros((POINTS, 0), jnp.float32)
    for block in range(BLOCKS):
        chosen = pivots[block]
        pivot_pts = points_t[:, chosen]
        pivot_rows = factor[chosen]
        pivot_block = kernel(pivot_pts, pivot_pts) - jnp.dot(pivot_rows.astype(jnp.float32), pivot_rows.T.astype(jnp.float32), precision=lax.Precision.HIGHEST, preferred_element_type=jnp.float32)
        lower = jnp.linalg.cholesky(pivot_block)
        inverse = jax.scipy.linalg.solve_triangular(lower, jnp.eye(PIV, dtype=jnp.float32), lower=True)
        factor_blocks = factor.reshape(nblocks, PTS_DEV, factor.shape[1])

        def one_block(pair):
            pts, rows = pair
            resid = kernel(pts, pivot_pts) - jnp.dot(rows.astype(jnp.float32), pivot_rows.T.astype(jnp.float32), precision=lax.Precision.HIGHEST, preferred_element_type=jnp.float32)
            return jnp.dot(resid.astype(jnp.float32), inverse.T.astype(jnp.float32), precision=lax.Precision.HIGHEST, preferred_element_type=jnp.float32)
        newcols = lax.map(one_block, (point_blocks, factor_blocks)).reshape(POINTS, PIV)
        factor = jnp.concatenate([factor, newcols], axis=1)
    residual_diag = 1.0 - jnp.sum(factor * factor, axis=1)
    return (factor.astype(jnp.bfloat16), residual_diag)
```

```python
import jax
import jax.numpy as jnp
from jax import lax
from jax.sharding import PartitionSpec as P


def kernel(left_t, right_t):
    cross = lax.dot_general(
        left_t,
        right_t,
        (((0,), (0,)), ((), ())),
        precision=lax.Precision.HIGHEST,
        preferred_element_type=jnp.float32,
    )
    sq = jnp.sum(left_t * left_t, 0)[:, None] + jnp.sum(right_t * right_t, 0)[None, :] - 2.0 * cross
    return jnp.exp(-sq / (1.65 * left_t.shape[0]))


def exact_dot(left, right):
    return jnp.dot(left, right, precision=lax.Precision.HIGHEST, preferred_element_type=jnp.float32)


def digits_of(ndev):
    rounds = []
    left = ndev
    while left > 1:
        radix = 4 if left % 8 == 0 else 2
        left //= radix
        rounds.append((radix, left))
    return rounds


def gather_relative(buffer, ndev):
    held = buffer[None]
    for radix, stride in digits_of(ndev):
        pieces = [held]
        for step in range(1, radix):
            pairs = []
            for d in range(ndev):
                digit = (d // stride) % radix
                pairs.append((d, d + ((digit + step) % radix - digit) * stride))
            pieces.append(lax.ppermute(held, "rows", pairs))
        held = jnp.concatenate(pieces, axis=0)
    return held


def place_of(owner, me, ndev):
    place = jnp.zeros_like(owner)
    scale = 1
    for radix, stride in digits_of(ndev):
        rel = (me // stride % radix - owner // stride % radix + radix) % radix
        place = place + rel * scale
        scale *= radix
    return place


def body(points_t, pivots):
    ndev = lax.axis_size("rows")
    dim, rows_here = points_t.shape
    blocks, piv = pivots.shape
    me = lax.axis_index("rows")
    capacity = piv // ndev + 2
    owner = pivots // rows_here
    earlier = lax.broadcasted_iota(jnp.int32, (piv, piv), 0) > lax.broadcasted_iota(
        jnp.int32, (piv, piv), 1
    )
    same = (owner[:, :, None] == owner[:, None, :]) & earlier[None]
    slot = jnp.sum(jnp.where(same, 1, 0), axis=2).astype(jnp.int32)
    slot_ids = lax.broadcasted_iota(jnp.int32, (blocks, capacity, piv), 1)
    hit = (slot_ids == slot[:, None, :]) & (owner[:, None, :] == me)
    column = jnp.sum(jnp.where(hit, (pivots - me * rows_here)[:, None, :] + 1, 0), axis=2) - 1
    col_ids = lax.broadcasted_iota(jnp.int32, (blocks, capacity, rows_here), 2)
    pick = jnp.where(col_ids == column[:, :, None], 1.0, 0.0).astype(jnp.float32)
    picked = lax.dot_general(
        pick.reshape(blocks * capacity, rows_here),
        points_t,
        (((1,), (1,)), ((), ())),
        precision=lax.Precision.HIGHEST,
        preferred_element_type=jnp.float32,
    ).reshape(blocks, capacity, dim)
    buffer = jnp.concatenate([picked[b] for b in range(blocks)], axis=1)
    gathered = gather_relative(buffer, ndev).reshape(ndev * capacity, blocks * dim)
    target = place_of(owner, me, ndev) * capacity + slot
    place_ids = lax.broadcasted_iota(jnp.int32, (blocks, ndev * capacity, piv), 1)
    placer = jnp.where(place_ids == target[:, None, :], 1.0, 0.0).astype(jnp.float32)
    pivot_pts = [
        lax.dot_general(
            gathered[:, b * dim : (b + 1) * dim],
            placer[b],
            (((0,), (0,)), ((), ())),
            precision=lax.Precision.HIGHEST,
            preferred_element_type=jnp.float32,
        )
        for b in range(blocks)
    ]

    eye_block = jnp.eye(piv, dtype=jnp.float32)
    factor = None
    inverses = []
    for block in range(blocks):
        resid = kernel(points_t, pivot_pts[block])
        pivot_block = kernel(pivot_pts[block], pivot_pts[block])
        if factor is not None:
            part = kernel(pivot_pts[block], pivot_pts[0])
            rows = exact_dot(part, inverses[0].T)
            resid = resid - exact_dot(factor, rows.T)
            pivot_block = pivot_block - exact_dot(rows, rows.T)
        lower = jnp.linalg.cholesky(pivot_block)
        inverse = jax.scipy.linalg.solve_triangular(lower, eye_block, lower=True)
        inverses.append(inverse)
        newcols = exact_dot(resid, inverse.T)
        factor = newcols if factor is None else jnp.concatenate([factor, newcols], axis=1)
    residual_diag = 1.0 - jnp.sum(factor * factor, axis=1)
    return (factor.astype(jnp.bfloat16), residual_diag)


def solution(mesh):
    return jax.shard_map(
        body,
        mesh=mesh,
        in_specs=(P(None, "rows"), P()),
        out_specs=(P("rows", None), P("rows")),
        check_vma=False,
    )
```

```python
import functools

import jax
import jax.numpy as jnp
from jax import lax
from jax.experimental import pallas as pl
from jax.experimental.pallas import tpu as pltpu
from jax.sharding import PartitionSpec as P

PANEL = 128
STEP = 8
LANES = 128


def halves(x):
    high = x.astype(jnp.bfloat16)
    return high, (x - high.astype(jnp.float32)).astype(jnp.bfloat16)


def thirds(x):
    high = x.astype(jnp.bfloat16)
    rest = x - high.astype(jnp.float32)
    mid, low = halves(rest)
    return high, mid, low


def nt_dot(left, right):
    return lax.dot_general(
        left, right, (((1,), (1,)), ((), ())), preferred_element_type=jnp.float32
    )


def left_form(x):
    high, low = halves(x)
    return jnp.concatenate([high, high, low], axis=1)


def right_form(x):
    high, low = halves(x)
    return jnp.concatenate([high, low, high], axis=1)


def exponent_operands(x, left, right):
    rows = x.shape[0]
    half = [-h for h in thirds(0.5 * jnp.sum(x * x, axis=1, keepdims=True))]
    one = jnp.ones((rows, 3), jnp.bfloat16)
    pad = jnp.zeros((rows, 256 - 3 * x.shape[1] - 6), jnp.bfloat16)
    high, low = halves(x)
    result = []
    if left:
        result.append(jnp.concatenate([high, high, low] + half + [one, pad], axis=1))
    if right:
        result.append(jnp.concatenate([high, low, high, one] + half + [pad], axis=1))
    return result


def lane_spread(x, lane):
    return jnp.broadcast_to(x[:, lane : lane + 1], (STEP, LANES))


def row_spread(x, row):
    return jnp.broadcast_to(x[row : row + 1, :], (STEP, LANES))


def panel_inverse(tiles):
    lane = lax.broadcasted_iota(jnp.int32, (STEP, LANES), 1)
    sub = lax.broadcasted_iota(jnp.int32, (STEP, LANES), 0)
    tiles = list(tiles)
    result = []
    for s in range(len(tiles)):
        first = STEP * s
        inside = (lane >= first) & (lane < first + STEP)
        cols = [lane_spread(tiles[s], first + k) for k in range(STEP)]
        e = {(i, k): row_spread(cols[k], i) for k in range(STEP) for i in range(k, STEP)}
        low = {}
        inv = []
        for k in range(STEP):
            inv.append(lax.rsqrt(e[k, k]))
            for i in range(k + 1, STEP):
                low[i, k] = e[i, k] * inv[k]
            for m in range(k + 1, STEP):
                for i in range(m, STEP):
                    e[i, m] = e[i, m] - low[i, k] * low[m, k]
        own = jnp.where(inside, jnp.where(lane - first == sub, 1.0, 0.0), tiles[s])
        upper = []
        for i in range(STEP):
            acc = row_spread(own, i)
            for m in range(i):
                acc = acc - low[i, m] * upper[m]
            upper.append(acc * inv[i])
        done = upper[0]
        for i in range(1, STEP):
            done = jnp.where(sub == i, upper[i], done)
        result.append(jnp.where(lane < first + STEP, done, 0.0))
        full = None
        for t in range(s + 1, len(tiles)):
            cols = [lane_spread(tiles[t], first + k) for k in range(STEP)]
            acc = jnp.where(inside, 0.0, tiles[t])
            if t == s + 1:
                mine = []
                for k in range(STEP):
                    col = cols[k]
                    for m in range(k):
                        col = col - low[k, m] * mine[m]
                    mine.append(col * inv[k])
                    acc = acc - mine[k] * upper[k]
            else:
                if full is None:
                    full = [None] * STEP
                    for i in reversed(range(STEP)):
                        back = upper[i]
                        for m in range(i + 1, STEP):
                            back = back - low[m, i] * full[m]
                        full[i] = back * inv[i]
                for k in range(STEP):
                    acc = acc - cols[k] * full[k]
            tiles[t] = acc
    return result


def factor_kernel(points_ref, pivots_ref, factor_ref, diag_ref, work, squares):
    rows = factor_ref.shape[0]
    width = factor_ref.shape[1]
    scale = (2.0 / (1.65 * pivots_ref.shape[1])) ** 0.5
    piv_left, piv_right = exponent_operands(pivots_ref[...] * scale, True, True)
    work[:width, :] = jnp.exp(nt_dot(piv_left, piv_right))
    work[width:, :] = jnp.exp(nt_dot(points_ref[...], piv_right))
    for first in range(0, width, PANEL):
        last = first + PANEL
        inverse = jnp.concatenate(
            panel_inverse(
                [work[first + r : first + r + STEP, first:last] for r in range(0, PANEL, STEP)]
            ),
            axis=0,
        )
        new = nt_dot(left_form(work[last:, first:last]), right_form(inverse))
        if last < width:
            below = new[: width - last]
            work[last:, last:] = work[last:, last:] - nt_dot(left_form(new), right_form(below))
        mine = new[width - last :]
        factor_ref[:, first:last] = mine.astype(jnp.bfloat16)
        squares[...] = mine * mine if first == 0 else squares[...] + mine * mine
    ones = jnp.ones((STEP, 3 * PANEL), jnp.bfloat16)
    sums = nt_dot(ones, jnp.concatenate(thirds(squares[...]), axis=1))
    diag_ref[...] = 1.0 - sums[:1]


def prepare_kernel(points_ref, out_ref):
    scale = (2.0 / (1.65 * points_ref.shape[0])) ** 0.5
    out_ref[...] = exponent_operands(points_ref[...].T * scale, True, False)[0]


VMEM = pl.BlockSpec(memory_space=pltpu.VMEM)


def prepare(points_t):
    return pl.pallas_call(
        prepare_kernel,
        out_shape=jax.ShapeDtypeStruct((points_t.shape[1], 256), jnp.bfloat16),
        in_specs=[VMEM],
        out_specs=VMEM,
        compiler_params=pltpu.CompilerParams(vmem_limit_bytes=32 * 2**20),
    )(points_t)


def factorize(points, pivot_pts):
    rows, width = points.shape[0], pivot_pts.shape[0]
    return pl.pallas_call(
        factor_kernel,
        out_shape=[
            jax.ShapeDtypeStruct((rows, width), jnp.bfloat16),
            jax.ShapeDtypeStruct((1, rows), jnp.float32),
        ],
        in_specs=[VMEM, VMEM],
        out_specs=[VMEM, VMEM],
        scratch_shapes=[
            pltpu.VMEM((width + rows, width), jnp.float32),
            pltpu.VMEM((rows, PANEL), jnp.float32),
        ],
        compiler_params=pltpu.CompilerParams(vmem_limit_bytes=48 * 2**20),
    )(points, pivot_pts)


def digits_of(ndev):
    rounds = []
    left = ndev
    while left > 1:
        radix = 4 if left % 8 == 0 else 2
        left //= radix
        rounds.append((radix, left))
    return rounds


def gather_relative(buffer, ndev):
    held = buffer[None]
    for radix, stride in digits_of(ndev):
        pieces = [held]
        for step in range(1, radix):
            pairs = []
            for d in range(ndev):
                digit = (d // stride) % radix
                pairs.append((d, d + ((digit + step) % radix - digit) * stride))
            pieces.append(lax.ppermute(held, "rows", pairs))
        held = jnp.concatenate(pieces, axis=0)
    return held


def place_of(owner, me, ndev):
    place = jnp.zeros_like(owner)
    scale = 1
    for radix, stride in digits_of(ndev):
        rel = (me // stride % radix - owner // stride % radix + radix) % radix
        place = place + rel * scale
        scale *= radix
    return place


def body(points_t, pivots):
    ndev = lax.axis_size("rows")
    dim, rows_here = points_t.shape
    blocks, piv = pivots.shape
    me = lax.axis_index("rows")
    capacity = piv // ndev + 2
    owner = pivots // rows_here
    earlier = lax.broadcasted_iota(jnp.int32, (piv, piv), 0) > lax.broadcasted_iota(
        jnp.int32, (piv, piv), 1
    )
    same = (owner[:, :, None] == owner[:, None, :]) & earlier[None]
    slot = jnp.sum(jnp.where(same, 1, 0), axis=2).astype(jnp.int32)
    slot_ids = lax.broadcasted_iota(jnp.int32, (blocks, capacity, piv), 1)
    hit = (slot_ids == slot[:, None, :]) & (owner[:, None, :] == me)
    column = jnp.sum(jnp.where(hit, (pivots - me * rows_here)[:, None, :] + 1, 0), axis=2) - 1
    col_ids = lax.broadcasted_iota(jnp.int32, (blocks, capacity, rows_here), 2)
    pick = jnp.where(col_ids == column[:, :, None], 1.0, 0.0).astype(jnp.float32)
    picked = lax.dot_general(
        pick.reshape(blocks * capacity, rows_here),
        points_t,
        (((1,), (1,)), ((), ())),
        precision=lax.Precision.HIGHEST,
        preferred_element_type=jnp.float32,
    ).reshape(blocks, capacity, dim)
    buffer = jnp.concatenate([picked[b] for b in range(blocks)], axis=1)
    gathered = gather_relative(buffer, ndev).reshape(ndev * capacity, blocks * dim)
    target = place_of(owner, me, ndev) * capacity + slot
    place_ids = lax.broadcasted_iota(jnp.int32, (blocks, ndev * capacity, piv), 1)
    placer = jnp.where(place_ids == target[:, None, :], 1.0, 0.0).astype(jnp.float32)
    pivot_pts = jnp.concatenate(
        [
            lax.dot_general(
                placer[b],
                gathered[:, b * dim : (b + 1) * dim],
                (((0,), (0,)), ((), ())),
                precision=lax.Precision.HIGHEST,
                preferred_element_type=jnp.float32,
            )
            for b in range(blocks)
        ],
        axis=0,
    )
    factor, diag = factorize(prepare(points_t), pivot_pts)
    return (factor, diag.reshape(rows_here))


def solution(mesh):
    return jax.shard_map(
        body,
        mesh=mesh,
        in_specs=(P(None, "rows"), P()),
        out_specs=(P("rows", None), P("rows")),
        check_vma=False,
    )
```

```python
import functools

import jax
import jax.numpy as jnp
from jax import lax
from jax.experimental import pallas as pl
from jax.experimental.pallas import tpu as pltpu
from jax.sharding import PartitionSpec as P

PANEL = 128
STEP = 8
LANES = 128
CHUNK = 128


def halves(x):
    high = x.astype(jnp.bfloat16)
    return high, (x - high.astype(jnp.float32)).astype(jnp.bfloat16)


def thirds(x):
    high = x.astype(jnp.bfloat16)
    mid, low = halves(x - high.astype(jnp.float32))
    return high, mid, low


def nn_dot(left, right):
    return jnp.dot(left, right, preferred_element_type=jnp.float32)


def nt_dot(left, right):
    return lax.dot_general(
        left, right, (((1,), (1,)), ((), ())), preferred_element_type=jnp.float32
    )


def left_form(x):
    high, low = halves(x)
    return jnp.concatenate([high, high, low], axis=1)


def right_form(x):
    high, low = halves(x)
    return jnp.concatenate([high, low, high], axis=1)


def exponent_operands(x, left, right):
    rows = x.shape[0]
    half = [-h for h in thirds(0.5 * jnp.sum(x * x, axis=1, keepdims=True))]
    one = jnp.ones((rows, 3), jnp.bfloat16)
    pad = jnp.zeros((rows, 256 - 3 * x.shape[1] - 6), jnp.bfloat16)
    high, low = halves(x)
    result = []
    if left:
        result.append(jnp.concatenate([high, high, low] + half + [one, pad], axis=1))
    if right:
        result.append(jnp.concatenate([high, low, high, one] + half + [pad], axis=1))
    return result


def lane_spread(x, lane):
    return jnp.broadcast_to(x[:, lane : lane + 1], (STEP, LANES))


def row_spread(x, row):
    return jnp.broadcast_to(x[row : row + 1, :], (STEP, LANES))


def small_factor(e):
    low = {}
    inv = {}
    for k in range(0, STEP, 2):
        det = e[k, k] * e[k + 1, k + 1] - e[k + 1, k] * e[k + 1, k]
        inv[k] = lax.rsqrt(e[k, k])
        inv[k + 1] = e[k, k] * lax.rsqrt(e[k, k] * det)
        low[k + 1, k] = e[k + 1, k] * inv[k]
        for i in range(k + 2, STEP):
            low[i, k] = e[i, k] * inv[k]
            low[i, k + 1] = (e[i, k + 1] - low[i, k] * low[k + 1, k]) * inv[k + 1]
        for m in range(k + 2, STEP):
            for i in range(m, STEP):
                e[i, m] = e[i, m] - low[i, k] * low[m, k] - low[i, k + 1] * low[m, k + 1]
    return low, inv


def panel_inverse(tiles, jobs):
    lane = lax.broadcasted_iota(jnp.int32, (STEP, LANES), 1)
    sub = lax.broadcasted_iota(jnp.int32, (STEP, LANES), 0)
    tiles = list(tiles)
    jobs = list(jobs)
    result = []
    for s in range(len(tiles)):
        first = STEP * s
        inside = (lane >= first) & (lane < first + STEP)
        cols = [lane_spread(tiles[s], first + k) for k in range(STEP)]
        e = {(i, k): row_spread(cols[k], i) for k in range(STEP) for i in range(k, STEP)}
        low, inv = small_factor(e)
        own = jnp.where(inside, jnp.where(lane - first == sub, 1.0, 0.0), tiles[s])
        upper = []
        for i in range(STEP):
            acc = row_spread(own, i)
            for m in range(i):
                acc = acc - low[i, m] * upper[m]
            upper.append(acc * inv[i])
        done = upper[0]
        for i in range(1, STEP):
            done = jnp.where(sub == i, upper[i], done)
        result.append(jnp.where(lane < first + STEP, done, 0.0))
        full = None
        for t in range(s + 1, len(tiles)):
            cols = [lane_spread(tiles[t], first + k) for k in range(STEP)]
            acc = jnp.where(inside, 0.0, tiles[t])
            if t == s + 1:
                mine = []
                for k in range(STEP):
                    col = cols[k]
                    for m in range(k):
                        col = col - low[k, m] * mine[m]
                    mine.append(col * inv[k])
                    acc = acc - mine[k] * upper[k]
            else:
                if full is None:
                    full = [None] * STEP
                    for i in reversed(range(STEP)):
                        back = upper[i]
                        for m in range(i + 1, STEP):
                            back = back - low[m, i] * full[m]
                        full[i] = back * inv[i]
                for k in range(STEP):
                    acc = acc - cols[k] * full[k]
            tiles[t] = acc
        if jobs:
            jobs.pop(0)()
    for job in jobs:
        job()
    return jnp.concatenate(result, axis=0)


def factor_kernel(points_ref, gathered_ref, target_ref, factor_ref, diag_ref, work, squares):
    rows, width = factor_ref.shape
    dim = gathered_ref.shape[1] // 2
    piv = width // 2
    scale = (2.0 / (1.65 * dim)) ** 0.5

    received = jnp.concatenate(thirds(gathered_ref[...] * scale), axis=1)
    target = target_ref[...].T
    place = lax.broadcasted_iota(jnp.int32, (piv, received.shape[0]), 1).astype(jnp.float32)
    parts = []
    for b in range(2):
        chosen = jnp.where(place == target[:, b : b + 1], 1.0, 0.0).astype(jnp.bfloat16)
        found = nn_dot(chosen, received)
        found = found[:, : 2 * dim] + found[:, 2 * dim : 4 * dim] + found[:, 4 * dim :]
        parts.append(found[:, b * dim : (b + 1) * dim])
    piv_left, piv_right = exponent_operands(jnp.concatenate(parts, axis=0), True, True)

    work[:width, :] = jnp.exp(nt_dot(piv_left, piv_right))

    def kernel_rows(first):
        def job():
            work[width + first : width + first + CHUNK, :] = jnp.exp(
                nt_dot(points_ref[first : first + CHUNK, :], piv_right)
            )

        return job

    def block_job(inverse, rights, block, start):
        def job():
            at = slice(block * PANEL, (block + 1) * PANEL)
            new = nt_dot(left_form(work[at, start : start + PANEL]), inverse)
            rights.append(right_form(new))
            left = left_form(new)
            for n, right in enumerate(rights):
                to = slice(start + PANEL * (n + 1), start + PANEL * (n + 2))
                work[at, to] = work[at, to] - nt_dot(left, right)

        return job

    def rows_job(inverse, rights, first, start):
        def job():
            at = slice(width + first, width + first + CHUNK)
            new = nt_dot(left_form(work[at, start : start + PANEL]), inverse)
            here = slice(first, first + CHUNK)
            factor_ref[here, start : start + PANEL] = new.astype(jnp.bfloat16)
            squares[here, :] = new * new if start == 0 else squares[here, :] + new * new
            if rights:
                work[at, start + PANEL :] = work[at, start + PANEL :] - nt_dot(
                    left_form(new), jnp.concatenate(rights, axis=0)
                )

        return job

    jobs = [kernel_rows(first) for first in range(0, rows, CHUNK)]
    for start in range(0, width, PANEL):
        block = slice(start, start + PANEL)
        inverse = right_form(
            panel_inverse([work[start + r : start + r + STEP, block] for r in range(0, PANEL, STEP)], jobs)
        )
        rights = []
        jobs = [
            block_job(inverse, rights, n, start)
            for n in range(start // PANEL + 1, width // PANEL)
        ]
        if jobs:
            jobs.pop(0)()
        jobs += [rows_job(inverse, rights, first, start) for first in range(0, rows, CHUNK)]
    for job in jobs:
        job()
    ones = jnp.ones((STEP, 3 * PANEL), jnp.bfloat16)
    sums = nt_dot(ones, jnp.concatenate(thirds(squares[...]), axis=1))
    diag_ref[...] = 1.0 - sums[:1]


def prepare_kernel(ndev, points_ref, pivots_ref, out_ref, buffer_ref, target_ref):
    dim, rows = points_ref.shape
    blocks, piv = pivots_ref.shape
    slots = buffer_ref.shape[1]
    me = lax.axis_index("rows")
    points = points_ref[...].T
    scale = (2.0 / (1.65 * dim)) ** 0.5
    out_ref[...] = exponent_operands(points * scale, True, False)[0]
    exact = jnp.concatenate(thirds(points), axis=1)
    before = jnp.where(
        lax.broadcasted_iota(jnp.int32, (piv, piv), 0)
        < lax.broadcasted_iota(jnp.int32, (piv, piv), 1),
        1.0,
        0.0,
    ).astype(jnp.bfloat16)
    device = lax.broadcasted_iota(jnp.int32, (ndev, piv), 0)
    targets = []
    picked = []
    for b in range(blocks):
        pivots = pivots_ref[b : b + 1, :]
        low = device * rows
        owned = jnp.where((pivots >= low) & (pivots < low + rows), 1.0, 0.0)
        count = nn_dot(owned.astype(jnp.bfloat16), before)
        slot = jnp.sum(owned * count, axis=0, keepdims=True)
        owner = jnp.sum(owned * device.astype(jnp.float32), axis=0, keepdims=True)
        targets.append(owner * slots + slot)
        local = pivots - me * rows
        mine = (local >= 0) & (local < rows)
        wanted = mine & (
            lax.broadcasted_iota(jnp.int32, (slots, piv), 0).astype(jnp.float32) == slot
        )
        column = jnp.sum(
            jnp.where(wanted, (local + 1).astype(jnp.float32), 0.0), axis=1, keepdims=True
        )
        place = lax.broadcasted_iota(jnp.int32, (slots, rows), 1).astype(jnp.float32)
        chosen = jnp.where(place + 1.0 == column, 1.0, 0.0).astype(jnp.bfloat16)
        found = nn_dot(chosen, exact)
        picked.append(found[:, :dim] + found[:, dim : 2 * dim] + found[:, 2 * dim :])
    buffer_ref[...] = jnp.broadcast_to(
        jnp.concatenate(picked, axis=1)[None], buffer_ref.shape
    )
    target_ref[...] = jnp.concatenate(
        targets + [jnp.zeros((STEP - blocks, piv), jnp.float32)], axis=0
    )


VMEM = pl.BlockSpec(memory_space=pltpu.VMEM)


def prepare(points_t, pivots, ndev, slots):
    dim, rows = points_t.shape
    return pl.pallas_call(
        functools.partial(prepare_kernel, ndev),
        out_shape=[
            jax.ShapeDtypeStruct((rows, 256), jnp.bfloat16),
            jax.ShapeDtypeStruct((ndev, slots, 2 * dim), jnp.float32),
            jax.ShapeDtypeStruct((STEP, pivots.shape[1]), jnp.float32),
        ],
        in_specs=[VMEM, VMEM],
        out_specs=[VMEM, VMEM, VMEM],
        compiler_params=pltpu.CompilerParams(vmem_limit_bytes=32 * 2**20),
    )(points_t, pivots)


def factorize(points, gathered, target, width):
    rows = points.shape[0]
    return pl.pallas_call(
        factor_kernel,
        out_shape=[
            jax.ShapeDtypeStruct((rows, width), jnp.bfloat16),
            jax.ShapeDtypeStruct((1, rows), jnp.float32),
        ],
        in_specs=[VMEM, VMEM, VMEM],
        out_specs=[VMEM, VMEM],
        scratch_shapes=[
            pltpu.VMEM((width + rows, width), jnp.float32),
            pltpu.VMEM((rows, PANEL), jnp.float32),
        ],
        compiler_params=pltpu.CompilerParams(vmem_limit_bytes=48 * 2**20),
    )(points, gathered, target)


def body(points_t, pivots):
    ndev = lax.axis_size("rows")
    dim, rows_here = points_t.shape
    blocks, piv = pivots.shape
    slots = -(-(piv // ndev + 2) // STEP) * STEP
    points, buffer, target = prepare(points_t, pivots, ndev, slots)
    gathered = lax.all_to_all(buffer, "rows", 0, 0, tiled=True)
    factor, diag = factorize(
        points, gathered.reshape(ndev * slots, blocks * dim), target, blocks * piv
    )
    return (factor, diag.reshape(rows_here))


def solution(mesh):
    return jax.shard_map(
        body,
        mesh=mesh,
        in_specs=(P(None, "rows"), P()),
        out_specs=(P("rows", None), P("rows")),
        check_vma=False,
    )
```

```python
import functools

import jax
import jax.numpy as jnp
from jax import lax
from jax.experimental import pallas as pl
from jax.experimental.pallas import tpu as pltpu
from jax.sharding import PartitionSpec as P

PANEL = 128
STEP = 8
LANES = 128
CHUNK = 128


def halves(x):
    high = x.astype(jnp.bfloat16)
    return high, (x - high.astype(jnp.float32)).astype(jnp.bfloat16)


def thirds(x):
    high = x.astype(jnp.bfloat16)
    mid, low = halves(x - high.astype(jnp.float32))
    return high, mid, low


def nn_dot(left, right):
    return jnp.dot(left, right, preferred_element_type=jnp.float32)


def nt_dot(left, right):
    return lax.dot_general(
        left, right, (((1,), (1,)), ((), ())), preferred_element_type=jnp.float32
    )


def left_form(x):
    high, low = halves(x)
    return jnp.concatenate([high, high, low], axis=1)


def right_form(x):
    high, low = halves(x)
    return jnp.concatenate([high, low, high], axis=1)


def exponent_operands(x, left, right):
    rows = x.shape[0]
    half = [-h for h in thirds(0.5 * jnp.sum(x * x, axis=1, keepdims=True))]
    one = jnp.ones((rows, 3), jnp.bfloat16)
    pad = jnp.zeros((rows, 256 - 3 * x.shape[1] - 6), jnp.bfloat16)
    high, low = halves(x)
    result = []
    if left:
        result.append(jnp.concatenate([high, high, low] + half + [one, pad], axis=1))
    if right:
        result.append(jnp.concatenate([high, low, high, one] + half + [pad], axis=1))
    return result


def lane_spread(x, lane):
    return jnp.broadcast_to(x[:, lane : lane + 1], (STEP, LANES))


def row_spread(x, row):
    return jnp.broadcast_to(x[row : row + 1, :], (STEP, LANES))


def small_factor(e):
    low = {}
    inv = {}
    for k in range(0, STEP, 2):
        a, b, c = e[k, k], e[k + 1, k], e[k + 1, k + 1]
        root = lax.rsqrt(a * c - b * b)
        inv[k] = lax.rsqrt(a)
        inv[k + 1] = (a * inv[k]) * root
        low[k + 1, k] = b * inv[k]
        over = root * root
        rest = range(k + 2, STEP)
        for i in rest:
            low[i, k] = e[i, k] * inv[k]
            low[i, k + 1] = (e[i, k + 1] - low[i, k] * low[k + 1, k]) * inv[k + 1]
        first = {i: c * e[i, k] - b * e[i, k + 1] for i in rest}
        second = {i: a * e[i, k + 1] - b * e[i, k] for i in rest}
        for m in rest:
            for i in range(m, STEP):
                e[i, m] = e[i, m] - (first[i] * e[m, k] + second[i] * e[m, k + 1]) * over
    return low, inv


def panel_inverse(tiles, jobs):
    lane = lax.broadcasted_iota(jnp.int32, (STEP, LANES), 1)
    sub = lax.broadcasted_iota(jnp.int32, (STEP, LANES), 0)
    tiles = list(tiles)
    jobs = list(jobs)
    result = []
    for s in range(len(tiles)):
        first = STEP * s
        inside = (lane >= first) & (lane < first + STEP)
        cols = [lane_spread(tiles[s], first + k) for k in range(STEP)]
        e = {(i, k): row_spread(cols[k], i) for k in range(STEP) for i in range(k, STEP)}
        low, inv = small_factor(e)
        own = jnp.where(inside, jnp.where(lane - first == sub, 1.0, 0.0), tiles[s])
        upper = []
        for i in range(STEP):
            acc = row_spread(own, i)
            for m in range(i):
                acc = acc - low[i, m] * upper[m]
            upper.append(acc * inv[i])
        done = upper[0]
        for i in range(1, STEP):
            done = jnp.where(sub == i, upper[i], done)
        result.append(jnp.where(lane < first + STEP, done, 0.0))
        full = None
        for t in range(s + 1, len(tiles)):
            cols = [lane_spread(tiles[t], first + k) for k in range(STEP)]
            acc = jnp.where(inside, 0.0, tiles[t])
            if t == s + 1:
                mine = []
                for k in range(STEP):
                    col = cols[k]
                    for m in range(k):
                        col = col - low[k, m] * mine[m]
                    mine.append(col * inv[k])
                    acc = acc - mine[k] * upper[k]
            else:
                if full is None:
                    full = [None] * STEP
                    for i in reversed(range(STEP)):
                        back = upper[i]
                        for m in range(i + 1, STEP):
                            back = back - low[m, i] * full[m]
                        full[i] = back * inv[i]
                for k in range(STEP):
                    acc = acc - cols[k] * full[k]
            tiles[t] = acc
        if jobs:
            jobs.pop(0)()
    for job in jobs:
        job()
    return jnp.concatenate(result, axis=0)


def factor_kernel(points_ref, near_ref, other_ref, target_ref, factor_ref, diag_ref, work, squares):
    rows, width = factor_ref.shape
    dim = near_ref.shape[1] // 2
    piv = width // 2
    scale = (2.0 / (1.65 * dim)) ** 0.5

    gathered = jnp.concatenate([near_ref[...], other_ref[...]], axis=0)
    received = jnp.concatenate(thirds(gathered * scale), axis=1)
    target = target_ref[...].T
    place = lax.broadcasted_iota(jnp.int32, (piv, received.shape[0]), 1).astype(jnp.float32)
    parts = []
    for b in range(2):
        chosen = jnp.where(place == target[:, b : b + 1], 1.0, 0.0).astype(jnp.bfloat16)
        found = nn_dot(chosen, received)
        found = found[:, : 2 * dim] + found[:, 2 * dim : 4 * dim] + found[:, 4 * dim :]
        parts.append(found[:, b * dim : (b + 1) * dim])
    piv_left, piv_right = exponent_operands(jnp.concatenate(parts, axis=0), True, True)

    def kernel_block(block):
        def job():
            first, last = block * PANEL, (block + 1) * PANEL
            work[first:last, :last] = jnp.exp(nt_dot(piv_left[first:last], piv_right[:last]))

        return job

    kernel_block(0)()

    def kernel_rows(first):
        def job():
            work[width + first : width + first + CHUNK, :] = jnp.exp(
                nt_dot(points_ref[first : first + CHUNK, :], piv_right)
            )

        return job

    def block_job(inverse, rights, block, start):
        def job():
            at = slice(block * PANEL, (block + 1) * PANEL)
            new = nt_dot(left_form(work[at, start : start + PANEL]), inverse)
            rights.append(right_form(new))
            left = left_form(new)
            for n, right in enumerate(rights):
                to = slice(start + PANEL * (n + 1), start + PANEL * (n + 2))
                work[at, to] = work[at, to] - nt_dot(left, right)

        return job

    def rows_job(inverse, rights, first, start):
        def job():
            at = slice(width + first, width + first + CHUNK)
            new = nt_dot(left_form(work[at, start : start + PANEL]), inverse)
            here = slice(first, first + CHUNK)
            factor_ref[here, start : start + PANEL] = new.astype(jnp.bfloat16)
            squares[here, :] = new * new if start == 0 else squares[here, :] + new * new
            if rights:
                work[at, start + PANEL :] = work[at, start + PANEL :] - nt_dot(
                    left_form(new), jnp.concatenate(rights, axis=0)
                )

        return job

    jobs = [kernel_block(block) for block in range(1, width // PANEL)]
    jobs += [kernel_rows(first) for first in range(0, rows, CHUNK)]
    for start in range(0, width, PANEL):
        block = slice(start, start + PANEL)
        inverse = right_form(
            panel_inverse([work[start + r : start + r + STEP, block] for r in range(0, PANEL, STEP)], jobs)
        )
        rights = []
        jobs = [
            block_job(inverse, rights, n, start)
            for n in range(start // PANEL + 1, width // PANEL)
        ]
        if jobs:
            jobs.pop(0)()
        jobs += [rows_job(inverse, rights, first, start) for first in range(0, rows, CHUNK)]
    for job in jobs:
        job()
    ones = jnp.ones((STEP, 3 * PANEL), jnp.bfloat16)
    sums = nt_dot(ones, jnp.concatenate(thirds(squares[...]), axis=1))
    diag_ref[...] = 1.0 - sums[:1]


def prepare_kernel(ndev, points_ref, pivots_ref, out_ref, buffer_ref, target_ref):
    dim, rows = points_ref.shape
    blocks, piv = pivots_ref.shape
    chips, slots = buffer_ref.shape[:2]
    me = lax.axis_index("rows")
    before = jnp.where(
        lax.broadcasted_iota(jnp.int32, (piv, piv), 0)
        < lax.broadcasted_iota(jnp.int32, (piv, piv), 1),
        1.0,
        0.0,
    ).astype(jnp.bfloat16)
    device = lax.broadcasted_iota(jnp.int32, (ndev, piv), 0)
    base = jnp.where(device % 2 == me % 2, 0, chips * slots) + device // 2 * slots
    targets = []
    columns = []
    for b in range(blocks):
        pivots = pivots_ref[b : b + 1, :]
        low = device * rows
        owned = jnp.where((pivots >= low) & (pivots < low + rows), 1.0, 0.0)
        count = nn_dot(owned.astype(jnp.bfloat16), before)
        slot = jnp.sum(owned * count, axis=0, keepdims=True)
        targets.append(slot + jnp.sum(owned * base.astype(jnp.float32), axis=0, keepdims=True))
        local = pivots - me * rows
        mine = (local >= 0) & (local < rows)
        wanted = mine & (
            lax.broadcasted_iota(jnp.int32, (slots, piv), 0).astype(jnp.float32) == slot
        )
        columns.append(
            jnp.sum(
                jnp.where(wanted, (local + 1).astype(jnp.float32), 0.0), axis=1, keepdims=True
            )
        )
    target_ref[...] = jnp.concatenate(
        targets + [jnp.zeros((STEP - blocks, piv), jnp.float32)], axis=0
    )
    points = points_ref[...].T
    scale = (2.0 / (1.65 * dim)) ** 0.5
    out_ref[...] = exponent_operands(points * scale, True, False)[0]
    exact = jnp.concatenate(thirds(points), axis=1)
    picked = []
    for column in columns:
        place = lax.broadcasted_iota(jnp.int32, (slots, rows), 1).astype(jnp.float32)
        chosen = jnp.where(place + 1.0 == column, 1.0, 0.0).astype(jnp.bfloat16)
        found = nn_dot(chosen, exact)
        picked.append(found[:, :dim] + found[:, dim : 2 * dim] + found[:, 2 * dim :])
    buffer_ref[...] = jnp.broadcast_to(
        jnp.concatenate(picked, axis=1)[None], buffer_ref.shape
    )


VMEM = pl.BlockSpec(memory_space=pltpu.VMEM)


def prepare(points_t, pivots, ndev, slots):
    dim, rows = points_t.shape
    return pl.pallas_call(
        functools.partial(prepare_kernel, ndev),
        out_shape=[
            jax.ShapeDtypeStruct((rows, 256), jnp.bfloat16),
            jax.ShapeDtypeStruct((ndev // 2, slots, 2 * dim), jnp.float32),
            jax.ShapeDtypeStruct((STEP, pivots.shape[1]), jnp.float32),
        ],
        in_specs=[VMEM] * 2,
        out_specs=[VMEM] * 3,
        compiler_params=pltpu.CompilerParams(vmem_limit_bytes=32 * 2**20),
    )(points_t, pivots)


def factorize(points, near, other, target, width):
    rows = points.shape[0]
    return pl.pallas_call(
        factor_kernel,
        out_shape=[
            jax.ShapeDtypeStruct((rows, width), jnp.bfloat16),
            jax.ShapeDtypeStruct((1, rows), jnp.float32),
        ],
        in_specs=[VMEM] * 4,
        out_specs=[VMEM] * 2,
        scratch_shapes=[
            pltpu.VMEM((width + rows, width), jnp.float32),
            pltpu.VMEM((rows, PANEL), jnp.float32),
        ],
        compiler_params=pltpu.CompilerParams(vmem_limit_bytes=48 * 2**20),
    )(points, near, other, target)


def body(points_t, pivots):
    ndev = lax.axis_size("rows")
    dim, rows_here = points_t.shape
    blocks, piv = pivots.shape
    slots = -(-(piv // ndev + 2) // STEP) * STEP
    points, buffer, target = prepare(points_t, pivots, ndev, slots)
    cores = [[d for d in range(ndev) if d % 2 == core] for core in range(2)]
    near = lax.all_to_all(buffer, "rows", 0, 0, axis_index_groups=cores, tiled=True)
    near = near.reshape(ndev // 2 * slots, blocks * dim)
    other = lax.ppermute(near, "rows", [(d, d ^ 1) for d in range(ndev)])
    factor, diag = factorize(points, near, other, target, blocks * piv)
    return (factor, diag.reshape(rows_here))


def solution(mesh):
    return jax.shard_map(
        body,
        mesh=mesh,
        in_specs=(P(None, "rows"), P()),
        out_specs=(P("rows", None), P("rows")),
        check_vma=False,
    )
```

```python
import functools

import jax
import jax.numpy as jnp
from jax import lax
from jax.experimental import pallas as pl
from jax.experimental.pallas import tpu as pltpu
from jax.sharding import PartitionSpec as P

PANEL = 128
STEP = 8
LANES = 128
CHUNK = 128


def halves(x):
    high = x.astype(jnp.bfloat16)
    return high, (x - high.astype(jnp.float32)).astype(jnp.bfloat16)


def thirds(x):
    high = x.astype(jnp.bfloat16)
    mid, low = halves(x - high.astype(jnp.float32))
    return high, mid, low


def nn_dot(left, right):
    return jnp.dot(left, right, preferred_element_type=jnp.float32)


def nt_dot(left, right):
    return lax.dot_general(
        left, right, (((1,), (1,)), ((), ())), preferred_element_type=jnp.float32
    )


def left_form(x):
    high, low = halves(x)
    return jnp.concatenate([high, high, low], axis=1)


def right_form(x):
    high, low = halves(x)
    return jnp.concatenate([high, low, high], axis=1)


def exponent_operands(x, left, right):
    rows = x.shape[0]
    half = [-h for h in thirds(0.5 * jnp.sum(x * x, axis=1, keepdims=True))]
    one = jnp.ones((rows, 3), jnp.bfloat16)
    pad = jnp.zeros((rows, 256 - 3 * x.shape[1] - 6), jnp.bfloat16)
    high, low = halves(x)
    result = []
    if left:
        result.append(jnp.concatenate([high, high, low] + half + [one, pad], axis=1))
    if right:
        result.append(jnp.concatenate([high, low, high, one] + half + [pad], axis=1))
    return result


def lane_spread(x, lane):
    return jnp.broadcast_to(x[:, lane : lane + 1], (STEP, LANES))


class Spreader:
    def __init__(self, ref):
        self.ref = ref
        self.at = 0

    def rows(self, x, first=0):
        base = self.at
        self.at += STEP
        self.ref[base : base + STEP, :] = x
        return {i: self.ref[pl.ds(base + i, STEP, stride=0), :] for i in range(first, STEP)}


def small_factor(e):
    low = {}
    inv = {}
    for k in range(0, STEP, 2):
        a, b, c = e[k, k], e[k + 1, k], e[k + 1, k + 1]
        root = lax.rsqrt(a * c - b * b)
        inv[k] = lax.rsqrt(a)
        inv[k + 1] = (a * inv[k]) * root
        low[k + 1, k] = b * inv[k]
        over = root * root
        rest = range(k + 2, STEP)
        for i in rest:
            low[i, k] = e[i, k] * inv[k]
            low[i, k + 1] = (e[i, k + 1] - low[i, k] * low[k + 1, k]) * inv[k + 1]
        first = {i: c * e[i, k] - b * e[i, k + 1] for i in rest}
        second = {i: a * e[i, k + 1] - b * e[i, k] for i in rest}
        for m in rest:
            for i in range(m, STEP):
                e[i, m] = e[i, m] - (first[i] * e[m, k] + second[i] * e[m, k + 1]) * over
    return low, inv


def panel_inverse(tiles, jobs, spread):
    lane = lax.broadcasted_iota(jnp.int32, (STEP, LANES), 1)
    sub = lax.broadcasted_iota(jnp.int32, (STEP, LANES), 0)
    tiles = list(tiles)
    jobs = list(jobs)
    result = []
    spreader = Spreader(spread)
    for s in range(len(tiles)):
        first = STEP * s
        inside = (lane >= first) & (lane < first + STEP)
        cols = [lane_spread(tiles[s], first + k) for k in range(STEP)]
        e = {}
        for k in range(STEP):
            for i, row in spreader.rows(cols[k], k).items():
                e[i, k] = row
        low, inv = small_factor(e)
        own = jnp.where(inside, jnp.where(lane - first == sub, 1.0, 0.0), tiles[s])
        upper = []
        own_rows = spreader.rows(own)
        for i in range(STEP):
            acc = own_rows[i]
            for m in range(i):
                acc = acc - low[i, m] * upper[m]
            upper.append(acc * inv[i])
        done = upper[0]
        for i in range(1, STEP):
            done = jnp.where(sub == i, upper[i], done)
        result.append(jnp.where(lane < first + STEP, done, 0.0))
        full = None
        for t in range(s + 1, len(tiles)):
            cols = [lane_spread(tiles[t], first + k) for k in range(STEP)]
            acc = jnp.where(inside, 0.0, tiles[t])
            if t == s + 1:
                mine = []
                for k in range(STEP):
                    col = cols[k]
                    for m in range(k):
                        col = col - low[k, m] * mine[m]
                    mine.append(col * inv[k])
                    acc = acc - mine[k] * upper[k]
            else:
                if full is None:
                    full = [None] * STEP
                    for i in reversed(range(STEP)):
                        back = upper[i]
                        for m in range(i + 1, STEP):
                            back = back - low[m, i] * full[m]
                        full[i] = back * inv[i]
                for k in range(STEP):
                    acc = acc - cols[k] * full[k]
            tiles[t] = acc
        if jobs:
            jobs.pop(0)()
    for job in jobs:
        job()
    return jnp.concatenate(result, axis=0)


def rounds_of(ndev):
    rounds = [(2, 1)]
    stride = 2
    while stride < ndev:
        radix = 4 if ndev // stride % 4 == 0 else 2
        rounds.append((radix, stride))
        stride *= radix
    return rounds[::-1]


def factor_kernel(points_ref, near_ref, other_ref, target_ref, factor_ref, diag_ref, work, squares, spread):
    rows, width = factor_ref.shape
    dim = near_ref.shape[1] // 2
    piv = width // 2
    scale = (2.0 / (1.65 * dim)) ** 0.5

    gathered = jnp.concatenate([near_ref[...], other_ref[...]], axis=0)
    received = jnp.concatenate(thirds(gathered * scale), axis=1)
    target = target_ref[...].T
    place = lax.broadcasted_iota(jnp.int32, (piv, received.shape[0]), 1).astype(jnp.float32)
    parts = []
    for b in range(2):
        chosen = jnp.where(place == target[:, b : b + 1], 1.0, 0.0).astype(jnp.bfloat16)
        found = nn_dot(chosen, received)
        found = found[:, : 2 * dim] + found[:, 2 * dim : 4 * dim] + found[:, 4 * dim :]
        parts.append(found[:, b * dim : (b + 1) * dim])
    piv_left, piv_right = exponent_operands(jnp.concatenate(parts, axis=0), True, True)

    def kernel_block(block):
        def job():
            first, last = block * PANEL, (block + 1) * PANEL
            work[first:last, :last] = jnp.exp(nt_dot(piv_left[first:last], piv_right[:last]))

        return job

    kernel_block(0)()

    def kernel_rows(first):
        def job():
            work[width + first : width + first + CHUNK, :] = jnp.exp(
                nt_dot(points_ref[first : first + CHUNK, :], piv_right)
            )

        return job

    def block_job(inverse, rights, block, start):
        def job():
            at = slice(block * PANEL, (block + 1) * PANEL)
            new = nt_dot(left_form(work[at, start : start + PANEL]), inverse)
            rights.append(right_form(new))
            left = left_form(new)
            for n, right in enumerate(rights):
                to = slice(start + PANEL * (n + 1), start + PANEL * (n + 2))
                work[at, to] = work[at, to] - nt_dot(left, right)

        return job

    def rows_job(inverse, rights, first, start):
        def job():
            at = slice(width + first, width + first + CHUNK)
            new = nt_dot(left_form(work[at, start : start + PANEL]), inverse)
            here = slice(first, first + CHUNK)
            factor_ref[here, start : start + PANEL] = new.astype(jnp.bfloat16)
            squares[here, :] = new * new if start == 0 else squares[here, :] + new * new
            if rights:
                work[at, start + PANEL :] = work[at, start + PANEL :] - nt_dot(
                    left_form(new), jnp.concatenate(rights, axis=0)
                )

        return job

    jobs = [kernel_block(block) for block in range(1, width // PANEL)]
    jobs += [kernel_rows(first) for first in range(0, rows, CHUNK)]
    for start in range(0, width, PANEL):
        block = slice(start, start + PANEL)
        inverse = right_form(
            panel_inverse(
                [work[start + r : start + r + STEP, block] for r in range(0, PANEL, STEP)],
                jobs,
                spread,
            )
        )
        rights = []
        jobs = [
            block_job(inverse, rights, n, start)
            for n in range(start // PANEL + 1, width // PANEL)
        ]
        if jobs:
            jobs.pop(0)()
        jobs += [rows_job(inverse, rights, first, start) for first in range(0, rows, CHUNK)]
    for job in jobs:
        job()
    ones = jnp.ones((STEP, 3 * PANEL), jnp.bfloat16)
    sums = nt_dot(ones, jnp.concatenate(thirds(squares[...]), axis=1))
    diag_ref[...] = 1.0 - sums[:1]


def prepare_kernel(ndev, points_ref, pivots_ref, out_ref, buffer_ref, target_ref):
    dim, rows = points_ref.shape
    blocks, piv = pivots_ref.shape
    slots = buffer_ref.shape[0]
    me = lax.axis_index("rows")
    before = jnp.where(
        lax.broadcasted_iota(jnp.int32, (piv, piv), 0)
        < lax.broadcasted_iota(jnp.int32, (piv, piv), 1),
        1.0,
        0.0,
    ).astype(jnp.bfloat16)
    device = lax.broadcasted_iota(jnp.int32, (ndev, piv), 0)
    base = jnp.zeros_like(device)
    scale = slots
    for radix, stride in rounds_of(ndev):
        base = base + ((device // stride) ^ (me // stride)) % radix * scale
        scale = scale * radix
    targets = []
    columns = []
    for b in range(blocks):
        pivots = pivots_ref[b : b + 1, :]
        low = device * rows
        owned = jnp.where((pivots >= low) & (pivots < low + rows), 1.0, 0.0)
        count = nn_dot(owned.astype(jnp.bfloat16), before)
        slot = jnp.sum(owned * count, axis=0, keepdims=True)
        targets.append(slot + jnp.sum(owned * base.astype(jnp.float32), axis=0, keepdims=True))
        local = pivots - me * rows
        mine = (local >= 0) & (local < rows)
        wanted = mine & (
            lax.broadcasted_iota(jnp.int32, (slots, piv), 0).astype(jnp.float32) == slot
        )
        columns.append(
            jnp.sum(
                jnp.where(wanted, (local + 1).astype(jnp.float32), 0.0), axis=1, keepdims=True
            )
        )
    target_ref[...] = jnp.concatenate(
        targets + [jnp.zeros((STEP - blocks, piv), jnp.float32)], axis=0
    )
    points = points_ref[...].T
    scale = (2.0 / (1.65 * dim)) ** 0.5
    out_ref[...] = exponent_operands(points * scale, True, False)[0]
    exact = jnp.concatenate(thirds(points), axis=1)
    picked = []
    for column in columns:
        place = lax.broadcasted_iota(jnp.int32, (slots, rows), 1).astype(jnp.float32)
        chosen = jnp.where(place + 1.0 == column, 1.0, 0.0).astype(jnp.bfloat16)
        found = nn_dot(chosen, exact)
        picked.append(found[:, :dim] + found[:, dim : 2 * dim] + found[:, 2 * dim :])
    buffer_ref[...] = jnp.concatenate(picked, axis=1)


VMEM = pl.BlockSpec(memory_space=pltpu.VMEM)


def prepare(points_t, pivots, ndev, slots):
    dim, rows = points_t.shape
    return pl.pallas_call(
        functools.partial(prepare_kernel, ndev),
        out_shape=[
            jax.ShapeDtypeStruct((rows, 256), jnp.bfloat16),
            jax.ShapeDtypeStruct((slots, 2 * dim), jnp.float32),
            jax.ShapeDtypeStruct((STEP, pivots.shape[1]), jnp.float32),
        ],
        in_specs=[VMEM] * 2,
        out_specs=[VMEM] * 3,
        compiler_params=pltpu.CompilerParams(vmem_limit_bytes=32 * 2**20),
    )(points_t, pivots)


def factorize(points, near, other, target, width):
    rows = points.shape[0]
    return pl.pallas_call(
        factor_kernel,
        out_shape=[
            jax.ShapeDtypeStruct((rows, width), jnp.bfloat16),
            jax.ShapeDtypeStruct((1, rows), jnp.float32),
        ],
        in_specs=[VMEM] * 4,
        out_specs=[VMEM] * 2,
        scratch_shapes=[
            pltpu.VMEM((width + rows, width), jnp.float32),
            pltpu.VMEM((rows, PANEL), jnp.float32),
            pltpu.VMEM(((STEP + 1) * PANEL, LANES), jnp.float32),
        ],
        compiler_params=pltpu.CompilerParams(vmem_limit_bytes=48 * 2**20),
    )(points, near, other, target)


def body(points_t, pivots):
    ndev = lax.axis_size("rows")
    dim, rows_here = points_t.shape
    blocks, piv = pivots.shape
    slots = -(-(piv // ndev + 2) // STEP) * STEP
    points, buffer, target = prepare(points_t, pivots, ndev, slots)
    held = buffer
    for radix, stride in rounds_of(ndev):
        pieces = [held]
        for step in range(1, radix):
            pairs = [(d, d ^ (step * stride)) for d in range(ndev)]
            pieces.append(lax.ppermute(held, "rows", pairs))
        if stride > 1:
            held = jnp.concatenate(pieces, axis=0)
    near, other = pieces
    factor, diag = factorize(points, near, other, target, blocks * piv)
    return (factor, diag.reshape(rows_here))


def solution(mesh):
    return jax.shard_map(
        body,
        mesh=mesh,
        in_specs=(P(None, "rows"), P()),
        out_specs=(P("rows", None), P("rows")),
        check_vma=False,
    )
```

```python
import functools

import jax
import jax.numpy as jnp
from jax import lax
from jax.experimental import pallas as pl
from jax.experimental.pallas import tpu as pltpu
from jax.sharding import PartitionSpec as P

PANEL = 128
STEP = 8
LANES = 128
CHUNK = 128


def halves(x):
    high = x.astype(jnp.bfloat16)
    return high, (x - high.astype(jnp.float32)).astype(jnp.bfloat16)


def thirds(x):
    high = x.astype(jnp.bfloat16)
    mid, low = halves(x - high.astype(jnp.float32))
    return high, mid, low


def nn_dot(left, right):
    return jnp.dot(left, right, preferred_element_type=jnp.float32)


def nt_dot(left, right):
    return lax.dot_general(
        left, right, (((1,), (1,)), ((), ())), preferred_element_type=jnp.float32
    )


def left_form(x):
    high, low = halves(x)
    return jnp.concatenate([high, high, low], axis=1)


def right_form(x):
    high, low = halves(x)
    return jnp.concatenate([high, low, high], axis=1)


def exponent_operands(x, left, right):
    rows = x.shape[0]
    half = [-h for h in thirds(0.5 * jnp.sum(x * x, axis=1, keepdims=True))]
    one = jnp.ones((rows, 3), jnp.bfloat16)
    pad = jnp.zeros((rows, 256 - 3 * x.shape[1] - 6), jnp.bfloat16)
    high, low = halves(x)
    result = []
    if left:
        result.append(jnp.concatenate([high, high, low] + half + [one, pad], axis=1))
    if right:
        result.append(jnp.concatenate([high, low, high, one] + half + [pad], axis=1))
    return result


def lane_spread(x, lane):
    return jnp.broadcast_to(x[:, lane : lane + 1], (STEP, LANES))


class Spreader:
    def __init__(self, ref):
        self.ref = ref
        self.at = 0

    def rows(self, x, first=0):
        base = self.at
        self.at += STEP
        self.ref[base : base + STEP, :] = x
        return {i: self.ref[pl.ds(base + i, STEP, stride=0), :] for i in range(first, STEP)}


def small_factor(e):
    low = {}
    inv = {}
    for k in range(0, STEP, 2):
        a, b, c = e[k, k], e[k + 1, k], e[k + 1, k + 1]
        root = lax.rsqrt(a * c - b * b)
        inv[k] = lax.rsqrt(a)
        inv[k + 1] = (a * inv[k]) * root
        low[k + 1, k] = b * inv[k]
        over = root * root
        rest = range(k + 2, STEP)
        for i in rest:
            low[i, k] = e[i, k] * inv[k]
            low[i, k + 1] = (e[i, k + 1] - low[i, k] * low[k + 1, k]) * inv[k + 1]
        first = {i: c * e[i, k] - b * e[i, k + 1] for i in rest}
        second = {i: a * e[i, k + 1] - b * e[i, k] for i in rest}
        for m in rest:
            for i in range(m, STEP):
                e[i, m] = e[i, m] - (first[i] * e[m, k] + second[i] * e[m, k + 1]) * over
    return low, inv


def panel_inverse(tiles, jobs, spread):
    lane = lax.broadcasted_iota(jnp.int32, (STEP, LANES), 1)
    sub = lax.broadcasted_iota(jnp.int32, (STEP, LANES), 0)
    tiles = list(tiles)
    jobs = list(jobs)
    result = []
    spreader = Spreader(spread)
    for s in range(len(tiles)):
        first = STEP * s
        inside = (lane >= first) & (lane < first + STEP)
        cols = [lane_spread(tiles[s], first + k) for k in range(STEP)]
        e = {}
        for k in range(STEP):
            for i, row in spreader.rows(cols[k], k).items():
                e[i, k] = row
        low, inv = small_factor(e)
        own = jnp.where(inside, jnp.where(lane - first == sub, 1.0, 0.0), tiles[s])
        upper = []
        own_rows = spreader.rows(own)
        for i in range(STEP):
            acc = own_rows[i]
            for m in range(i):
                acc = acc - low[i, m] * upper[m]
            upper.append(acc * inv[i])
        done = upper[0]
        for i in range(1, STEP):
            done = jnp.where(sub == i, upper[i], done)
        result.append(jnp.where(lane < first + STEP, done, 0.0))
        full = None
        for t in range(s + 1, len(tiles)):
            cols = [lane_spread(tiles[t], first + k) for k in range(STEP)]
            acc = jnp.where(inside, 0.0, tiles[t])
            if t == s + 1:
                mine = []
                for k in range(STEP):
                    col = cols[k]
                    for m in range(k):
                        col = col - low[k, m] * mine[m]
                    mine.append(col * inv[k])
                    acc = acc - mine[k] * upper[k]
            else:
                if full is None:
                    full = [None] * STEP
                    for i in reversed(range(STEP)):
                        back = upper[i]
                        for m in range(i + 1, STEP):
                            back = back - low[m, i] * full[m]
                        full[i] = back * inv[i]
                for k in range(STEP):
                    acc = acc - cols[k] * full[k]
            tiles[t] = acc
        if jobs:
            jobs.pop(0)()
    for job in jobs:
        job()
    return jnp.concatenate(result, axis=0)


def factor_kernel(points_ref, near_ref, other_ref, target_ref, factor_ref, diag_ref, work, squares, spread):
    rows, width = factor_ref.shape
    dim = near_ref.shape[1] // 2
    piv = width // 2
    scale = (2.0 / (1.65 * dim)) ** 0.5

    gathered = jnp.concatenate([near_ref[...], other_ref[...]], axis=0)
    received = jnp.concatenate(thirds(gathered * scale), axis=1)
    target = target_ref[...].T
    place = lax.broadcasted_iota(jnp.int32, (PANEL, received.shape[0]), 1).astype(jnp.float32)
    piv_left = []
    piv_right = []

    def kernel_block(block):
        def job():
            first = block * PANEL
            half, at = divmod(first, piv)
            chosen = jnp.where(place == target[at : at + PANEL, half : half + 1], 1.0, 0.0)
            found = nn_dot(chosen.astype(jnp.bfloat16), received)
            found = found[:, : 2 * dim] + found[:, 2 * dim : 4 * dim] + found[:, 4 * dim :]
            left, right = exponent_operands(found[:, half * dim : (half + 1) * dim], True, True)
            piv_left.append(left)
            piv_right.append(right)
            for n in range(block + 1):
                work[first : first + PANEL, n * PANEL : (n + 1) * PANEL] = jnp.exp(
                    nt_dot(left, piv_right[n])
                )

        return job

    kernel_block(0)()

    def kernel_rows(first, pair):
        def job():
            right = jnp.concatenate(piv_right[2 * pair : 2 * pair + 2], axis=0)
            cols = slice(2 * pair * PANEL, 2 * (pair + 1) * PANEL)
            here = slice(first, first + 2 * CHUNK)
            work[width + first : width + first + 2 * CHUNK, cols] = jnp.exp(
                nt_dot(points_ref[here, :], right)
            )

        return job

    def block_job(inverse, rights, block, start):
        def job():
            at = slice(block * PANEL, (block + 1) * PANEL)
            new = nt_dot(left_form(work[at, start : start + PANEL]), inverse)
            rights.append(right_form(new))
            left = left_form(new)
            for n, right in enumerate(rights):
                to = slice(start + PANEL * (n + 1), start + PANEL * (n + 2))
                work[at, to] = work[at, to] - nt_dot(left, right)

        return job

    def rows_job(inverse, rights, first, start):
        def job():
            at = slice(width + first, width + first + CHUNK)
            new = nt_dot(left_form(work[at, start : start + PANEL]), inverse)
            here = slice(first, first + CHUNK)
            factor_ref[here, start : start + PANEL] = new.astype(jnp.bfloat16)
            squares[here, :] = new * new if start == 0 else squares[here, :] + new * new
            if rights:
                work[at, start + PANEL :] = work[at, start + PANEL :] - nt_dot(
                    left_form(new), jnp.concatenate(rights, axis=0)
                )

        return job

    jobs = [kernel_block(block) for block in range(1, width // PANEL)]
    jobs += [
        kernel_rows(first, pair)
        for pair in range(width // PANEL // 2)
        for first in range(0, rows, 2 * CHUNK)
    ]
    for start in range(0, width, PANEL):
        block = slice(start, start + PANEL)
        inverse = right_form(
            panel_inverse(
                [work[start + r : start + r + STEP, block] for r in range(0, PANEL, STEP)],
                jobs,
                spread,
            )
        )
        rights = []
        jobs = [
            block_job(inverse, rights, n, start)
            for n in range(start // PANEL + 1, width // PANEL)
        ]
        if jobs:
            jobs.pop(0)()
        jobs += [rows_job(inverse, rights, first, start) for first in range(0, rows, CHUNK)]
    for job in jobs:
        job()
    ones = jnp.ones((3 * PANEL, LANES), jnp.bfloat16)
    keep = lax.broadcasted_iota(jnp.int32, (LANES, LANES), 0) == lax.broadcasted_iota(
        jnp.int32, (LANES, LANES), 1
    )
    for first in range(0, rows, LANES):
        here = slice(first, first + LANES)
        sums = nn_dot(jnp.concatenate(thirds(squares[here, :]), axis=1), ones)
        diag_ref[:, here] = 1.0 - jnp.sum(jnp.where(keep, sums, 0.0), axis=0, keepdims=True)


def slots_kernel(ndev, rows, slots, pivots_ref, target_ref, column_ref):
    blocks, piv = pivots_ref.shape
    me = lax.axis_index("rows")
    before = jnp.where(
        lax.broadcasted_iota(jnp.int32, (piv, piv), 0)
        < lax.broadcasted_iota(jnp.int32, (piv, piv), 1),
        1.0,
        0.0,
    ).astype(jnp.bfloat16)
    device = lax.broadcasted_iota(jnp.int32, (ndev, piv), 0)
    base = jnp.where(device % 2 == me % 2, 0, ndev // 2 * slots) + device // 2 * slots
    targets = []
    columns = []
    for b in range(blocks):
        pivots = pivots_ref[b : b + 1, :]
        low = device * rows
        owned = jnp.where((pivots >= low) & (pivots < low + rows), 1.0, 0.0)
        count = nn_dot(owned.astype(jnp.bfloat16), before)
        slot = jnp.sum(owned * count, axis=0, keepdims=True)
        targets.append(slot + jnp.sum(owned * base.astype(jnp.float32), axis=0, keepdims=True))
        local = pivots - me * rows
        mine = (local >= 0) & (local < rows)
        wanted = mine & (
            lax.broadcasted_iota(jnp.int32, (slots, piv), 0).astype(jnp.float32) == slot
        )
        columns.append(
            jnp.sum(
                jnp.where(wanted, (local + 1).astype(jnp.float32), 0.0), axis=1, keepdims=True
            )
        )
    target_ref[...] = jnp.concatenate(
        targets + [jnp.zeros((STEP - blocks, piv), jnp.float32)], axis=0
    )
    for b in range(blocks):
        column_ref[b * slots : (b + 1) * slots, :] = jnp.broadcast_to(columns[b], (slots, LANES))


def prepare_kernel(points_ref, column_ref, out_ref, buffer_ref):
    dim, rows = points_ref.shape
    slots = buffer_ref.shape[1]
    points = points_ref[...].T
    scale = (2.0 / (1.65 * dim)) ** 0.5
    out_ref[...] = exponent_operands(points * scale, True, False)[0]
    place = lax.broadcasted_iota(jnp.int32, (column_ref.shape[0], rows), 1).astype(jnp.float32)
    chosen = jnp.where(place + 1.0 == column_ref[:, :1], 1.0, 0.0).astype(jnp.bfloat16)
    found = nn_dot(chosen, jnp.concatenate(thirds(points), axis=1))
    found = found[:, :dim] + found[:, dim : 2 * dim] + found[:, 2 * dim :]
    picked = jnp.concatenate([found[:slots], found[slots:]], axis=1)
    buffer_ref[...] = jnp.broadcast_to(picked[None], buffer_ref.shape)


VMEM = pl.BlockSpec(memory_space=pltpu.VMEM)


def prepare(points_t, pivots, ndev, slots):
    dim, rows = points_t.shape
    blocks, piv = pivots.shape
    target, column = pl.pallas_call(
        functools.partial(slots_kernel, ndev, rows, slots),
        out_shape=[
            jax.ShapeDtypeStruct((STEP, piv), jnp.float32),
            jax.ShapeDtypeStruct((blocks * slots, LANES), jnp.float32),
        ],
        in_specs=[VMEM],
        out_specs=[VMEM] * 2,
        compiler_params=pltpu.CompilerParams(vmem_limit_bytes=32 * 2**20),
        cost_estimate=pl.CostEstimate(
            flops=4 * blocks * piv * piv * ndev, bytes_accessed=3 * 2**20, transcendentals=0
        ),
    )(pivots)
    points, buffer = pl.pallas_call(
        prepare_kernel,
        out_shape=[
            jax.ShapeDtypeStruct((rows, 256), jnp.bfloat16),
            jax.ShapeDtypeStruct((ndev // 2, slots, blocks * dim), jnp.float32),
        ],
        in_specs=[VMEM] * 2,
        out_specs=[VMEM] * 2,
        compiler_params=pltpu.CompilerParams(vmem_limit_bytes=32 * 2**20),
    )(points_t, column)
    return points, buffer, target


def factorize(points, near, other, target, width):
    rows = points.shape[0]
    return pl.pallas_call(
        factor_kernel,
        out_shape=[
            jax.ShapeDtypeStruct((rows, width), jnp.bfloat16),
            jax.ShapeDtypeStruct((1, rows), jnp.float32),
        ],
        in_specs=[VMEM] * 4,
        out_specs=[VMEM] * 2,
        scratch_shapes=[
            pltpu.VMEM((width + rows, width), jnp.float32),
            pltpu.VMEM((rows, PANEL), jnp.float32),
            pltpu.VMEM(((STEP + 1) * PANEL, LANES), jnp.float32),
        ],
        compiler_params=pltpu.CompilerParams(vmem_limit_bytes=48 * 2**20),
    )(points, near, other, target)


def body(points_t, pivots):
    ndev = lax.axis_size("rows")
    dim, rows_here = points_t.shape
    blocks, piv = pivots.shape
    slots = -(-(piv // ndev + 2) // STEP) * STEP
    points, buffer, target = prepare(points_t, pivots, ndev, slots)
    cores = [[d for d in range(ndev) if d % 2 == core] for core in range(2)]
    near = lax.all_to_all(buffer, "rows", 0, 0, axis_index_groups=cores, tiled=True)
    near = near.reshape(ndev // 2 * slots, blocks * dim)
    other = lax.ppermute(near, "rows", [(d, d ^ 1) for d in range(ndev)])
    factor, diag = factorize(points, near, other, target, blocks * piv)
    return (factor, diag.reshape(rows_here))


def solution(mesh):
    return jax.shard_map(
        body,
        mesh=mesh,
        in_specs=(P(None, "rows"), P()),
        out_specs=(P("rows", None), P("rows")),
        check_vma=False,
    )
```

```python
import functools

import jax
import jax.numpy as jnp
from jax import lax
from jax.experimental import pallas as pl
from jax.experimental.pallas import tpu as pltpu
from jax.sharding import PartitionSpec as P

PANEL = 128
STEP = 8
LANES = 128
CHUNK = 128


def halves(x):
    high = x.astype(jnp.bfloat16)
    return high, (x - high.astype(jnp.float32)).astype(jnp.bfloat16)


def thirds(x):
    high = x.astype(jnp.bfloat16)
    mid, low = halves(x - high.astype(jnp.float32))
    return high, mid, low


def nn_dot(left, right):
    return jnp.dot(left, right, preferred_element_type=jnp.float32)


def nt_dot(left, right):
    return lax.dot_general(
        left, right, (((1,), (1,)), ((), ())), preferred_element_type=jnp.float32
    )


def left_form(x):
    high, low = halves(x)
    return jnp.concatenate([high, high, low], axis=1)


def right_form(x):
    high, low = halves(x)
    return jnp.concatenate([high, low, high], axis=1)


def exponent_operands(x, left, right):
    rows = x.shape[0]
    half = [-h for h in thirds(0.5 * jnp.sum(x * x, axis=1, keepdims=True))]
    one = jnp.ones((rows, 3), jnp.bfloat16)
    pad = jnp.zeros((rows, 256 - 3 * x.shape[1] - 6), jnp.bfloat16)
    high, low = halves(x)
    result = []
    if left:
        result.append(jnp.concatenate([high, high, low] + half + [one, pad], axis=1))
    if right:
        result.append(jnp.concatenate([high, low, high, one] + half + [pad], axis=1))
    return result


def lane_spread(x, lane):
    return jnp.broadcast_to(x[:, lane : lane + 1], (STEP, LANES))


class Spreader:
    def __init__(self, ref):
        self.ref = ref
        self.at = 0

    def rows(self, x, first=0):
        base = self.at
        self.at += STEP
        self.ref[base : base + STEP, :] = x
        return {i: self.ref[pl.ds(base + i, STEP, stride=0), :] for i in range(first, STEP)}


def small_factor(e):
    low = {}
    inv = {}
    for k in range(0, STEP, 2):
        a, b, c = e[k, k], e[k + 1, k], e[k + 1, k + 1]
        root = lax.rsqrt(a * c - b * b)
        inv[k] = lax.rsqrt(a)
        inv[k + 1] = (a * inv[k]) * root
        low[k + 1, k] = b * inv[k]
        for i in range(k + 2, STEP):
            low[i, k] = e[i, k] * inv[k]
            low[i, k + 1] = (e[i, k + 1] - low[i, k] * low[k + 1, k]) * inv[k + 1]
        for m in range(k + 2, STEP):
            for i in range(m, STEP):
                e[i, m] = (e[i, m] - low[i, k] * low[m, k]) - low[i, k + 1] * low[m, k + 1]
    return low, inv


def panel_inverse(tiles, jobs, spread):
    lane = lax.broadcasted_iota(jnp.int32, (STEP, LANES), 1)
    sub = lax.broadcasted_iota(jnp.int32, (STEP, LANES), 0)
    tiles = list(tiles)
    jobs = list(jobs)
    result = []
    spreader = Spreader(spread)
    for s in range(len(tiles)):
        first = STEP * s
        inside = (lane >= first) & (lane < first + STEP)
        cols = [lane_spread(tiles[s], first + k) for k in range(STEP)]
        e = {}
        for k in range(STEP):
            for i, row in spreader.rows(cols[k], k).items():
                e[i, k] = row
        low, inv = small_factor(e)
        own = jnp.where(inside, jnp.where(lane - first == sub, 1.0, 0.0), tiles[s])
        upper = []
        own_rows = spreader.rows(own)
        for i in range(STEP):
            acc = own_rows[i]
            for m in range(i):
                acc = acc - low[i, m] * upper[m]
            upper.append(acc * inv[i])
        done = upper[0]
        for i in range(1, STEP):
            done = jnp.where(sub == i, upper[i], done)
        result.append(jnp.where(lane < first + STEP, done, 0.0))
        full = None
        for t in range(s + 1, len(tiles)):
            cols = [lane_spread(tiles[t], first + k) for k in range(STEP)]
            acc = jnp.where(inside, 0.0, tiles[t])
            if t == s + 1:
                mine = []
                for k in range(STEP):
                    col = cols[k]
                    for m in range(k):
                        col = col - low[k, m] * mine[m]
                    mine.append(col * inv[k])
                    acc = acc - mine[k] * upper[k]
            else:
                if full is None:
                    full = [None] * STEP
                    for i in reversed(range(STEP)):
                        back = upper[i]
                        for m in range(i + 1, STEP):
                            back = back - low[m, i] * full[m]
                        full[i] = back * inv[i]
                for k in range(STEP):
                    acc = acc - cols[k] * full[k]
            tiles[t] = acc
        if jobs:
            jobs.pop(0)()
    for job in jobs:
        job()
    return jnp.concatenate(result, axis=0)


def factor_kernel(points_ref, near_ref, other_ref, target_ref, factor_ref, diag_ref, work, squares, spread):
    rows, width = factor_ref.shape
    dim = near_ref.shape[1] // 2
    piv = width // 2
    scale = (2.0 / (1.65 * dim)) ** 0.5

    gathered = jnp.concatenate([near_ref[...], other_ref[...]], axis=0)
    received = jnp.concatenate(thirds(gathered * scale), axis=1)
    target = target_ref[...].T
    place = lax.broadcasted_iota(jnp.int32, (PANEL, received.shape[0]), 1).astype(jnp.float32)
    piv_left = []
    piv_right = []

    def kernel_block(block):
        def job():
            first = block * PANEL
            half, at = divmod(first, piv)
            chosen = jnp.where(place == target[at : at + PANEL, half : half + 1], 1.0, 0.0)
            found = nn_dot(chosen.astype(jnp.bfloat16), received)
            found = found[:, : 2 * dim] + found[:, 2 * dim : 4 * dim] + found[:, 4 * dim :]
            left, right = exponent_operands(found[:, half * dim : (half + 1) * dim], True, True)
            piv_left.append(left)
            piv_right.append(right)
            for n in range(block + 1):
                work[first : first + PANEL, n * PANEL : (n + 1) * PANEL] = jnp.exp(
                    nt_dot(left, piv_right[n])
                )

        return job

    kernel_block(0)()

    def kernel_rows(first, pair):
        def job():
            right = jnp.concatenate(piv_right[2 * pair : 2 * pair + 2], axis=0)
            cols = slice(2 * pair * PANEL, 2 * (pair + 1) * PANEL)
            here = slice(first, first + 2 * CHUNK)
            work[width + first : width + first + 2 * CHUNK, cols] = jnp.exp(
                nt_dot(points_ref[here, :], right)
            )

        return job

    def block_job(inverse, rights, block, start):
        def job():
            at = slice(block * PANEL, (block + 1) * PANEL)
            new = nt_dot(left_form(work[at, start : start + PANEL]), inverse)
            rights.append(right_form(new))
            left = left_form(new)
            for n, right in enumerate(rights):
                to = slice(start + PANEL * (n + 1), start + PANEL * (n + 2))
                work[at, to] = work[at, to] - nt_dot(left, right)

        return job

    def rows_job(inverse, rights, first, start):
        def job():
            at = slice(width + first, width + first + CHUNK)
            new = nt_dot(left_form(work[at, start : start + PANEL]), inverse)
            here = slice(first, first + CHUNK)
            factor_ref[here, start : start + PANEL] = new.astype(jnp.bfloat16)
            squares[here, :] = new * new if start == 0 else squares[here, :] + new * new
            if rights:
                work[at, start + PANEL :] = work[at, start + PANEL :] - nt_dot(
                    left_form(new), jnp.concatenate(rights, axis=0)
                )

        return job

    jobs = [kernel_block(block) for block in range(1, width // PANEL)]
    jobs += [
        kernel_rows(first, pair)
        for pair in range(width // PANEL // 2)
        for first in range(0, rows, 2 * CHUNK)
    ]
    for start in range(0, width, PANEL):
        block = slice(start, start + PANEL)
        inverse = right_form(
            panel_inverse(
                [work[start + r : start + r + STEP, block] for r in range(0, PANEL, STEP)],
                jobs,
                spread,
            )
        )
        rights = []
        jobs = [
            block_job(inverse, rights, n, start)
            for n in range(start // PANEL + 1, width // PANEL)
        ]
        if jobs:
            jobs.pop(0)()
        jobs += [rows_job(inverse, rights, first, start) for first in range(0, rows, CHUNK)]
    for job in jobs:
        job()
    ones = jnp.ones((3 * PANEL, LANES), jnp.bfloat16)
    keep = lax.broadcasted_iota(jnp.int32, (LANES, LANES), 0) == lax.broadcasted_iota(
        jnp.int32, (LANES, LANES), 1
    )
    for first in range(0, rows, LANES):
        here = slice(first, first + LANES)
        sums = nn_dot(jnp.concatenate(thirds(squares[here, :]), axis=1), ones)
        diag_ref[:, here] = 1.0 - jnp.sum(jnp.where(keep, sums, 0.0), axis=0, keepdims=True)


def slots_kernel(ndev, rows, slots, pivots_ref, target_ref, column_ref):
    blocks, piv = pivots_ref.shape
    me = lax.axis_index("rows")
    before = jnp.where(
        lax.broadcasted_iota(jnp.int32, (piv, piv), 0)
        < lax.broadcasted_iota(jnp.int32, (piv, piv), 1),
        1.0,
        0.0,
    ).astype(jnp.bfloat16)
    device = lax.broadcasted_iota(jnp.int32, (ndev, piv), 0)
    base = jnp.where(device % 2 == me % 2, 0, ndev // 2 * slots) + device // 2 * slots
    targets = []
    columns = []
    for b in range(blocks):
        pivots = pivots_ref[b : b + 1, :]
        low = device * rows
        owned = jnp.where((pivots >= low) & (pivots < low + rows), 1.0, 0.0)
        count = nn_dot(owned.astype(jnp.bfloat16), before)
        slot = jnp.sum(owned * count, axis=0, keepdims=True)
        targets.append(slot + jnp.sum(owned * base.astype(jnp.float32), axis=0, keepdims=True))
        local = pivots - me * rows
        mine = (local >= 0) & (local < rows)
        wanted = mine & (
            lax.broadcasted_iota(jnp.int32, (slots, piv), 0).astype(jnp.float32) == slot
        )
        columns.append(
            jnp.sum(
                jnp.where(wanted, (local + 1).astype(jnp.float32), 0.0), axis=1, keepdims=True
            )
        )
    target_ref[...] = jnp.concatenate(
        targets + [jnp.zeros((STEP - blocks, piv), jnp.float32)], axis=0
    )
    for b in range(blocks):
        column_ref[b * slots : (b + 1) * slots, :] = jnp.broadcast_to(columns[b], (slots, LANES))


def points_kernel(points_ref, out_ref):
    scale = (2.0 / (1.65 * points_ref.shape[0])) ** 0.5
    out_ref[...] = exponent_operands(points_ref[...].T * scale, True, False)[0]


def pick_kernel(points_ref, column_ref, buffer_ref):
    dim, rows = points_ref.shape
    slots = buffer_ref.shape[1]
    place = lax.broadcasted_iota(jnp.int32, (column_ref.shape[0], rows), 1).astype(jnp.float32)
    chosen = jnp.where(place + 1.0 == column_ref[:, :1], 1.0, 0.0).astype(jnp.bfloat16)
    found = nt_dot(chosen, jnp.concatenate(thirds(points_ref[...]), axis=0))
    found = found[:, :dim] + found[:, dim : 2 * dim] + found[:, 2 * dim :]
    picked = jnp.concatenate([found[:slots], found[slots:]], axis=1)
    buffer_ref[...] = jnp.broadcast_to(picked[None], buffer_ref.shape)


VMEM = pl.BlockSpec(memory_space=pltpu.VMEM)


def prepare(points_t, pivots, ndev, slots):
    dim, rows = points_t.shape
    blocks, piv = pivots.shape
    target, column = pl.pallas_call(
        functools.partial(slots_kernel, ndev, rows, slots),
        out_shape=[
            jax.ShapeDtypeStruct((STEP, piv), jnp.float32),
            jax.ShapeDtypeStruct((blocks * slots, LANES), jnp.float32),
        ],
        in_specs=[VMEM],
        out_specs=[VMEM] * 2,
        compiler_params=pltpu.CompilerParams(vmem_limit_bytes=32 * 2**20),
    )(pivots)
    buffer = pl.pallas_call(
        pick_kernel,
        out_shape=jax.ShapeDtypeStruct((ndev // 2, slots, blocks * dim), jnp.float32),
        in_specs=[VMEM] * 2,
        out_specs=VMEM,
        compiler_params=pltpu.CompilerParams(vmem_limit_bytes=32 * 2**20),
    )(points_t, column)
    points = pl.pallas_call(
        points_kernel,
        out_shape=jax.ShapeDtypeStruct((rows, 256), jnp.bfloat16),
        in_specs=[VMEM],
        out_specs=VMEM,
        compiler_params=pltpu.CompilerParams(vmem_limit_bytes=32 * 2**20),
        cost_estimate=pl.CostEstimate(
            flops=20 * rows * dim, bytes_accessed=3 * rows * 256, transcendentals=0
        ),
    )(points_t)
    return points, buffer, target


def factorize(points, near, other, target, width):
    rows = points.shape[0]
    return pl.pallas_call(
        factor_kernel,
        out_shape=[
            jax.ShapeDtypeStruct((rows, width), jnp.bfloat16),
            jax.ShapeDtypeStruct((1, rows), jnp.float32),
        ],
        in_specs=[VMEM] * 4,
        out_specs=[VMEM] * 2,
        scratch_shapes=[
            pltpu.VMEM((width + rows, width), jnp.float32),
            pltpu.VMEM((rows, PANEL), jnp.float32),
            pltpu.VMEM(((STEP + 1) * PANEL, LANES), jnp.float32),
        ],
        compiler_params=pltpu.CompilerParams(vmem_limit_bytes=48 * 2**20),
    )(points, near, other, target)


def body(points_t, pivots):
    ndev = lax.axis_size("rows")
    dim, rows_here = points_t.shape
    blocks, piv = pivots.shape
    slots = -(-(piv // ndev + 2) // STEP) * STEP
    points, buffer, target = prepare(points_t, pivots, ndev, slots)
    cores = [[d for d in range(ndev) if d % 2 == core] for core in range(2)]
    near = lax.all_to_all(buffer, "rows", 0, 0, axis_index_groups=cores, tiled=True)
    near = near.reshape(ndev // 2 * slots, blocks * dim)
    other = lax.ppermute(near, "rows", [(d, d ^ 1) for d in range(ndev)])
    factor, diag = factorize(points, near, other, target, blocks * piv)
    return (factor, diag.reshape(rows_here))


def solution(mesh):
    return jax.shard_map(
        body,
        mesh=mesh,
        in_specs=(P(None, "rows"), P()),
        out_specs=(P("rows", None), P("rows")),
        check_vma=False,
    )
```

```python
import functools

import jax
import jax.numpy as jnp
from jax import lax
from jax.experimental import pallas as pl
from jax.experimental.pallas import tpu as pltpu
from jax.sharding import PartitionSpec as P

PANEL = 128
STEP = 8
LANES = 128
CHUNK = 128


def halves(x):
    high = x.astype(jnp.bfloat16)
    return high, (x - high.astype(jnp.float32)).astype(jnp.bfloat16)


def thirds(x):
    high = x.astype(jnp.bfloat16)
    mid, low = halves(x - high.astype(jnp.float32))
    return high, mid, low


def nn_dot(left, right):
    return jnp.dot(left, right, preferred_element_type=jnp.float32)


def nt_dot(left, right):
    return lax.dot_general(
        left, right, (((1,), (1,)), ((), ())), preferred_element_type=jnp.float32
    )


def left_form(x):
    high, low = halves(x)
    return jnp.concatenate([high, high, low], axis=1)


def right_form(x):
    high, low = halves(x)
    return jnp.concatenate([high, low, high], axis=1)


def exponent_operands(x, left, right):
    rows = x.shape[0]
    half = [-h for h in thirds(0.5 * jnp.sum(x * x, axis=1, keepdims=True))]
    one = jnp.ones((rows, 3), jnp.bfloat16)
    pad = jnp.zeros((rows, 256 - 3 * x.shape[1] - 6), jnp.bfloat16)
    high, low = halves(x)
    result = []
    if left:
        result.append(jnp.concatenate([high, high, low] + half + [one, pad], axis=1))
    if right:
        result.append(jnp.concatenate([high, low, high, one] + half + [pad], axis=1))
    return result


def lane_spread(x, lane):
    return jnp.broadcast_to(x[:, lane : lane + 1], (STEP, LANES))


class Spreader:
    def __init__(self, ref):
        self.ref = ref
        self.at = 0

    def rows(self, x, first=0):
        base = self.at
        self.at += STEP
        self.ref[base : base + STEP, :] = x
        return {i: self.ref[pl.ds(base + i, STEP, stride=0), :] for i in range(first, STEP)}


def small_factor(e):
    low = {}
    inv = {}
    for k in range(0, STEP, 2):
        a, b, c = e[k, k], e[k + 1, k], e[k + 1, k + 1]
        root = lax.rsqrt(a * c - b * b)
        inv[k] = lax.rsqrt(a)
        inv[k + 1] = (a * inv[k]) * root
        low[k + 1, k] = b * inv[k]
        over = root * root
        rest = {}
        for i in range(k + 2, STEP):
            low[i, k] = e[i, k] * inv[k]
            rest[i] = e[i, k + 1] - low[i, k] * low[k + 1, k]
            low[i, k + 1] = rest[i] * inv[k + 1]
        for m in range(k + 2, STEP):
            for i in range(m, STEP):
                e[i, m] = e[i, m] - low[i, k] * low[m, k]
                if i < k + 4:
                    e[i, m] = e[i, m] - (rest[i] * (a * rest[m])) * over
                else:
                    e[i, m] = e[i, m] - low[i, k + 1] * low[m, k + 1]
    return low, inv, a, over


def panel_inverse(tiles, jobs, spread):
    lane = lax.broadcasted_iota(jnp.int32, (STEP, LANES), 1)
    sub = lax.broadcasted_iota(jnp.int32, (STEP, LANES), 0)
    tiles = list(tiles)
    jobs = list(jobs)
    result = []
    spreader = Spreader(spread)
    for s in range(len(tiles)):
        first = STEP * s
        inside = (lane >= first) & (lane < first + STEP)
        cols = [lane_spread(tiles[s], first + k) for k in range(STEP)]
        e = {}
        for k in range(STEP):
            for i, row in spreader.rows(cols[k], k).items():
                e[i, k] = row
        low, inv, pivot, over = small_factor(e)
        own = jnp.where(inside, jnp.where(lane - first == sub, 1.0, 0.0), tiles[s])
        upper = []
        own_rows = spreader.rows(own)
        for i in range(STEP):
            acc = own_rows[i]
            for m in range(i):
                acc = acc - low[i, m] * upper[m]
            upper.append(acc * inv[i])
            last_row = acc
        done = upper[0]
        for i in range(1, STEP):
            done = jnp.where(sub == i, upper[i], done)
        result.append(jnp.where(lane < first + STEP, done, 0.0))
        full = None
        for t in range(s + 1, len(tiles)):
            cols = [lane_spread(tiles[t], first + k) for k in range(STEP)]
            acc = jnp.where(inside, 0.0, tiles[t])
            if t == s + 1:
                mine = []
                for k in range(STEP):
                    col = cols[k]
                    for m in range(k):
                        col = col - low[k, m] * mine[m]
                    mine.append(col * inv[k])
                    if k < STEP - 1:
                        acc = acc - mine[k] * upper[k]
                    else:
                        acc = acc - (col * (pivot * last_row)) * over
            else:
                if full is None:
                    full = [None] * STEP
                    for i in reversed(range(STEP)):
                        back = upper[i]
                        for m in range(i + 1, STEP):
                            back = back - low[m, i] * full[m]
                        full[i] = back * inv[i]
                for k in range(STEP):
                    acc = acc - cols[k] * full[k]
            tiles[t] = acc
        if jobs:
            jobs.pop(0)()
    for job in jobs:
        job()
    return jnp.concatenate(result, axis=0)


def factor_kernel(
    points_ref,
    near_ref,
    other_ref,
    target_ref,
    factor_hbm,
    diag_ref,
    work,
    squares,
    spread,
    factor_ref,
    sems,
):
    rows, width = factor_ref.shape
    dim = near_ref.shape[1] // 2
    piv = width // 2
    scale = (2.0 / (1.65 * dim)) ** 0.5

    gathered = jnp.concatenate([near_ref[...], other_ref[...]], axis=0)
    received = jnp.concatenate(thirds(gathered * scale), axis=1)
    target = target_ref[...].T
    place = lax.broadcasted_iota(jnp.int32, (PANEL, received.shape[0]), 1).astype(jnp.float32)
    piv_left = []
    piv_right = []
    copies = []

    def kernel_block(block):
        def job():
            first = block * PANEL
            half, at = divmod(first, piv)
            chosen = jnp.where(place == target[at : at + PANEL, half : half + 1], 1.0, 0.0)
            found = nn_dot(chosen.astype(jnp.bfloat16), received)
            found = found[:, : 2 * dim] + found[:, 2 * dim : 4 * dim] + found[:, 4 * dim :]
            left, right = exponent_operands(found[:, half * dim : (half + 1) * dim], True, True)
            piv_left.append(left)
            piv_right.append(right)
            for n in range(block + 1):
                work[first : first + PANEL, n * PANEL : (n + 1) * PANEL] = jnp.exp(
                    nt_dot(left, piv_right[n])
                )

        return job

    kernel_block(0)()

    def kernel_rows(first, pair):
        def job():
            right = jnp.concatenate(piv_right[2 * pair : 2 * pair + 2], axis=0)
            cols = slice(2 * pair * PANEL, 2 * (pair + 1) * PANEL)
            here = slice(first, first + 2 * CHUNK)
            work[width + first : width + first + 2 * CHUNK, cols] = jnp.exp(
                nt_dot(points_ref[here, :], right)
            )

        return job

    def block_job(inverse, rights, block, start):
        def job():
            at = slice(block * PANEL, (block + 1) * PANEL)
            new = nt_dot(left_form(work[at, start : start + PANEL]), inverse)
            rights.append(right_form(new))
            left = left_form(new)
            for n, right in enumerate(rights):
                to = slice(start + PANEL * (n + 1), start + PANEL * (n + 2))
                work[at, to] = work[at, to] - nt_dot(left, right)

        return job

    def rows_job(inverse, rights, first, start):
        def job():
            at = slice(width + first, width + first + CHUNK)
            new = nt_dot(left_form(work[at, start : start + PANEL]), inverse)
            here = slice(first, first + CHUNK)
            factor_ref[here, start : start + PANEL] = new.astype(jnp.bfloat16)
            squares[here, :] = new * new if start == 0 else squares[here, :] + new * new
            if first + CHUNK == rows:
                cols = slice(start, start + PANEL)
                copies.append(
                    pltpu.make_async_copy(
                        factor_ref.at[:, cols], factor_hbm.at[:, cols], sems.at[start // PANEL]
                    )
                )
                copies[-1].start()
            if rights:
                work[at, start + PANEL :] = work[at, start + PANEL :] - nt_dot(
                    left_form(new), jnp.concatenate(rights, axis=0)
                )

        return job

    jobs = [kernel_block(block) for block in range(1, width // PANEL)]
    jobs += [
        kernel_rows(first, pair)
        for pair in range(width // PANEL // 2)
        for first in range(0, rows, 2 * CHUNK)
    ]
    for start in range(0, width, PANEL):
        block = slice(start, start + PANEL)
        inverse = right_form(
            panel_inverse(
                [work[start + r : start + r + STEP, block] for r in range(0, PANEL, STEP)],
                jobs,
                spread,
            )
        )
        rights = []
        jobs = [
            block_job(inverse, rights, n, start)
            for n in range(start // PANEL + 1, width // PANEL)
        ]
        if jobs:
            jobs.pop(0)()
        jobs += [rows_job(inverse, rights, first, start) for first in range(0, rows, CHUNK)]
    for job in jobs:
        job()
    ones = jnp.ones((3 * PANEL, LANES), jnp.bfloat16)
    keep = lax.broadcasted_iota(jnp.int32, (LANES, LANES), 0) == lax.broadcasted_iota(
        jnp.int32, (LANES, LANES), 1
    )
    for first in range(0, rows, LANES):
        here = slice(first, first + LANES)
        sums = nn_dot(jnp.concatenate(thirds(squares[here, :]), axis=1), ones)
        diag_ref[:, here] = 1.0 - jnp.sum(jnp.where(keep, sums, 0.0), axis=0, keepdims=True)
    for copy in copies:
        copy.wait()


def slots_kernel(ndev, rows, slots, pivots_ref, target_ref, column_ref):
    blocks, piv = pivots_ref.shape
    me = lax.axis_index("rows")
    before = jnp.where(
        lax.broadcasted_iota(jnp.int32, (piv, piv), 0)
        < lax.broadcasted_iota(jnp.int32, (piv, piv), 1),
        1.0,
        0.0,
    ).astype(jnp.bfloat16)
    device = lax.broadcasted_iota(jnp.int32, (ndev, piv), 0)
    base = jnp.where(device % 2 == me % 2, 0, ndev // 2 * slots) + device // 2 * slots
    targets = []
    columns = []
    for b in range(blocks):
        pivots = pivots_ref[b : b + 1, :]
        low = device * rows
        owned = jnp.where((pivots >= low) & (pivots < low + rows), 1.0, 0.0)
        count = nn_dot(owned.astype(jnp.bfloat16), before)
        slot = jnp.sum(owned * count, axis=0, keepdims=True)
        targets.append(slot + jnp.sum(owned * base.astype(jnp.float32), axis=0, keepdims=True))
        local = pivots - me * rows
        mine = (local >= 0) & (local < rows)
        wanted = mine & (
            lax.broadcasted_iota(jnp.int32, (slots, piv), 0).astype(jnp.float32) == slot
        )
        columns.append(
            jnp.sum(
                jnp.where(wanted, (local + 1).astype(jnp.float32), 0.0), axis=1, keepdims=True
            )
        )
    target_ref[...] = jnp.concatenate(
        targets + [jnp.zeros((STEP - blocks, piv), jnp.float32)], axis=0
    )
    for b in range(blocks):
        column_ref[b * slots : (b + 1) * slots, :] = jnp.broadcast_to(columns[b], (slots, LANES))


def points_kernel(points_ref, out_ref):
    scale = (2.0 / (1.65 * points_ref.shape[0])) ** 0.5
    out_ref[...] = exponent_operands(points_ref[...].T * scale, True, False)[0]


def pick_kernel(points_ref, column_ref, buffer_ref):
    dim, rows = points_ref.shape
    slots = buffer_ref.shape[1]
    place = lax.broadcasted_iota(jnp.int32, (column_ref.shape[0], rows), 1).astype(jnp.float32)
    chosen = jnp.where(place + 1.0 == column_ref[:, :1], 1.0, 0.0).astype(jnp.bfloat16)
    found = nt_dot(chosen, jnp.concatenate(thirds(points_ref[...]), axis=0))
    found = found[:, :dim] + found[:, dim : 2 * dim] + found[:, 2 * dim :]
    picked = jnp.concatenate([found[:slots], found[slots:]], axis=1)
    buffer_ref[...] = jnp.broadcast_to(picked[None], buffer_ref.shape)


VMEM = pl.BlockSpec(memory_space=pltpu.VMEM)


def prepare(points_t, pivots, ndev, slots):
    dim, rows = points_t.shape
    blocks, piv = pivots.shape
    target, column = pl.pallas_call(
        functools.partial(slots_kernel, ndev, rows, slots),
        out_shape=[
            jax.ShapeDtypeStruct((STEP, piv), jnp.float32),
            jax.ShapeDtypeStruct((blocks * slots, LANES), jnp.float32),
        ],
        in_specs=[VMEM],
        out_specs=[VMEM] * 2,
        compiler_params=pltpu.CompilerParams(vmem_limit_bytes=32 * 2**20),
    )(pivots)
    buffer = pl.pallas_call(
        pick_kernel,
        out_shape=jax.ShapeDtypeStruct((ndev // 2, slots, blocks * dim), jnp.float32),
        in_specs=[VMEM] * 2,
        out_specs=VMEM,
        compiler_params=pltpu.CompilerParams(vmem_limit_bytes=32 * 2**20),
    )(points_t, column)
    points = pl.pallas_call(
        points_kernel,
        out_shape=jax.ShapeDtypeStruct((rows, 256), jnp.bfloat16),
        in_specs=[VMEM],
        out_specs=VMEM,
        compiler_params=pltpu.CompilerParams(vmem_limit_bytes=32 * 2**20),
        cost_estimate=pl.CostEstimate(
            flops=20 * rows * dim, bytes_accessed=3 * rows * 256, transcendentals=0
        ),
    )(points_t)
    return points, buffer, target


def factorize(points, near, other, target, width):
    rows = points.shape[0]
    return pl.pallas_call(
        factor_kernel,
        out_shape=[
            jax.ShapeDtypeStruct((rows, width), jnp.bfloat16),
            jax.ShapeDtypeStruct((1, rows), jnp.float32),
        ],
        in_specs=[VMEM] * 4,
        out_specs=[pl.BlockSpec(memory_space=pl.ANY), VMEM],
        scratch_shapes=[
            pltpu.VMEM((width + rows, width), jnp.float32),
            pltpu.VMEM((rows, PANEL), jnp.float32),
            pltpu.VMEM(((STEP + 1) * PANEL, LANES), jnp.float32),
            pltpu.VMEM((rows, width), jnp.bfloat16),
            pltpu.SemaphoreType.DMA((width // PANEL,)),
        ],
        compiler_params=pltpu.CompilerParams(vmem_limit_bytes=48 * 2**20),
    )(points, near, other, target)


def body(points_t, pivots):
    ndev = lax.axis_size("rows")
    dim, rows_here = points_t.shape
    blocks, piv = pivots.shape
    slots = -(-(piv // ndev + 2) // STEP) * STEP
    points, buffer, target = prepare(points_t, pivots, ndev, slots)
    cores = [[d for d in range(ndev) if d % 2 == core] for core in range(2)]
    near = lax.all_to_all(buffer, "rows", 0, 0, axis_index_groups=cores, tiled=True)
    near = near.reshape(ndev // 2 * slots, blocks * dim)
    other = lax.ppermute(near, "rows", [(d, d ^ 1) for d in range(ndev)])
    factor, diag = factorize(points, near, other, target, blocks * piv)
    return (factor, diag.reshape(rows_here))


def solution(mesh):
    return jax.shard_map(
        body,
        mesh=mesh,
        in_specs=(P(None, "rows"), P()),
        out_specs=(P("rows", None), P("rows")),
        check_vma=False,
    )
```

```python
import functools

import jax
import jax.numpy as jnp
from jax import lax
from jax.experimental import pallas as pl
from jax.experimental.pallas import tpu as pltpu
from jax.sharding import PartitionSpec as P

PANEL = 128
STEP = 8
LANES = 128
CHUNK = 512


def halves(x):
    high = x.astype(jnp.bfloat16)
    return high, (x - high.astype(jnp.float32)).astype(jnp.bfloat16)


def thirds(x):
    high = x.astype(jnp.bfloat16)
    mid, low = halves(x - high.astype(jnp.float32))
    return high, mid, low


def nn_dot(left, right):
    return jnp.dot(left, right, preferred_element_type=jnp.float32)


def nt_dot(left, right):
    return lax.dot_general(
        left, right, (((1,), (1,)), ((), ())), preferred_element_type=jnp.float32
    )


def left_form(x):
    high, low = halves(x)
    return jnp.concatenate([high, high, low], axis=1)


def right_form(x):
    high, low = halves(x)
    return jnp.concatenate([high, low, high], axis=1)


def exponent_operands(x, left, right):
    rows = x.shape[0]
    half = [-h for h in thirds(0.5 * jnp.sum(x * x, axis=1, keepdims=True))]
    one = jnp.ones((rows, 3), jnp.bfloat16)
    pad = jnp.zeros((rows, 256 - 3 * x.shape[1] - 6), jnp.bfloat16)
    high, low = halves(x)
    result = []
    if left:
        result.append(jnp.concatenate([high, high, low] + half + [one, pad], axis=1))
    if right:
        result.append(jnp.concatenate([high, low, high, one] + half + [pad], axis=1))
    return result


def lane_spread(x, lane):
    return jnp.broadcast_to(x[:, lane : lane + 1], (STEP, LANES))


class Spreader:
    def __init__(self, ref):
        self.ref = ref
        self.at = 0

    def rows(self, x, first=0):
        base = self.at
        self.at += STEP
        self.ref[base : base + STEP, :] = x
        return {i: self.ref[pl.ds(base + i, STEP, stride=0), :] for i in range(first, STEP)}


def small_factor(e):
    low = {}
    inv = {}
    for k in range(0, STEP, 2):
        a, b, c = e[k, k], e[k + 1, k], e[k + 1, k + 1]
        root = lax.rsqrt(a * c - b * b)
        inv[k] = lax.rsqrt(a)
        inv[k + 1] = (a * inv[k]) * root
        low[k + 1, k] = b * inv[k]
        for i in range(k + 2, STEP):
            low[i, k] = e[i, k] * inv[k]
            low[i, k + 1] = (e[i, k + 1] - low[i, k] * low[k + 1, k]) * inv[k + 1]
        for m in range(k + 2, STEP):
            for i in range(m, STEP):
                e[i, m] = (e[i, m] - low[i, k] * low[m, k]) - low[i, k + 1] * low[m, k + 1]
    return low, inv


def panel_inverse(tiles, jobs, spread):
    lane = lax.broadcasted_iota(jnp.int32, (STEP, LANES), 1)
    sub = lax.broadcasted_iota(jnp.int32, (STEP, LANES), 0)
    tiles = list(tiles)
    jobs = list(jobs)
    result = []
    spreader = Spreader(spread)
    for s in range(len(tiles)):
        first = STEP * s
        inside = (lane >= first) & (lane < first + STEP)
        cols = [lane_spread(tiles[s], first + k) for k in range(STEP)]
        e = {}
        for k in range(STEP):
            for i, row in spreader.rows(cols[k], k).items():
                e[i, k] = row
        low, inv = small_factor(e)
        own = jnp.where(inside, jnp.where(lane - first == sub, 1.0, 0.0), tiles[s])
        upper = []
        own_rows = spreader.rows(own)
        for i in range(STEP):
            acc = own_rows[i]
            for m in range(i):
                acc = acc - low[i, m] * upper[m]
            upper.append(acc * inv[i])
        done = upper[0]
        for i in range(1, STEP):
            done = jnp.where(sub == i, upper[i], done)
        result.append(jnp.where(lane < first + STEP, done, 0.0))
        full = None
        for t in range(s + 1, len(tiles)):
            cols = [lane_spread(tiles[t], first + k) for k in range(STEP)]
            acc = jnp.where(inside, 0.0, tiles[t])
            if t == s + 1:
                mine = []
                for k in range(STEP):
                    col = cols[k]
                    for m in range(k):
                        col = col - low[k, m] * mine[m]
                    mine.append(col * inv[k])
                    acc = acc - mine[k] * upper[k]
            else:
                if full is None:
                    full = [None] * STEP
                    for i in reversed(range(STEP)):
                        back = upper[i]
                        for m in range(i + 1, STEP):
                            back = back - low[m, i] * full[m]
                        full[i] = back * inv[i]
                for k in range(STEP):
                    acc = acc - cols[k] * full[k]
            tiles[t] = acc
        if jobs:
            jobs.pop(0)()
    for job in jobs:
        job()
    return jnp.concatenate(result, axis=0)


def factor_kernel(points_ref, near_ref, other_ref, target_ref, factor_ref, diag_ref, work, squares, spread):
    rows, width = factor_ref.shape
    dim = near_ref.shape[1] // 2
    piv = width // 2
    scale = (2.0 / (1.65 * dim)) ** 0.5

    gathered = jnp.concatenate([near_ref[...], other_ref[...]], axis=0)
    received = jnp.concatenate(thirds(gathered * scale), axis=1)
    target = target_ref[...].T
    place = lax.broadcasted_iota(jnp.int32, (PANEL, received.shape[0]), 1).astype(jnp.float32)
    piv_left = []
    piv_right = []

    def kernel_block(block):
        def job():
            first = block * PANEL
            half, at = divmod(first, piv)
            chosen = jnp.where(place == target[at : at + PANEL, half : half + 1], 1.0, 0.0)
            found = nn_dot(chosen.astype(jnp.bfloat16), received)
            found = found[:, : 2 * dim] + found[:, 2 * dim : 4 * dim] + found[:, 4 * dim :]
            left, right = exponent_operands(found[:, half * dim : (half + 1) * dim], True, True)
            piv_left.append(left)
            piv_right.append(right)
            for n in range(block + 1):
                work[first : first + PANEL, n * PANEL : (n + 1) * PANEL] = jnp.exp(
                    nt_dot(left, piv_right[n])
                )

        return job

    kernel_block(0)()

    def kernel_rows(first, pair):
        def job():
            right = jnp.concatenate(piv_right[2 * pair : 2 * pair + 2], axis=0)
            cols = slice(2 * pair * PANEL, 2 * (pair + 1) * PANEL)
            here = slice(first, first + 2 * CHUNK)
            work[width + first : width + first + 2 * CHUNK, cols] = jnp.exp(
                nt_dot(points_ref[here, :], right)
            )

        return job

    def block_job(inverse, rights, block, start):
        def job():
            at = slice(block * PANEL, (block + 1) * PANEL)
            new = nt_dot(left_form(work[at, start : start + PANEL]), inverse)
            rights.append(right_form(new))
            left = left_form(new)
            for n, right in enumerate(rights):
                to = slice(start + PANEL * (n + 1), start + PANEL * (n + 2))
                work[at, to] = work[at, to] - nt_dot(left, right)

        return job

    def rows_job(inverse, rights, first, start):
        def job():
            at = slice(width + first, width + first + CHUNK)
            new = nt_dot(left_form(work[at, start : start + PANEL]), inverse)
            here = slice(first, first + CHUNK)
            factor_ref[here, start : start + PANEL] = new.astype(jnp.bfloat16)
            squares[here, :] = new * new if start == 0 else squares[here, :] + new * new
            if rights:
                work[at, start + PANEL :] = work[at, start + PANEL :] - nt_dot(
                    left_form(new), jnp.concatenate(rights, axis=0)
                )

        return job

    jobs = [kernel_block(block) for block in range(1, width // PANEL)]
    jobs += [
        kernel_rows(first, pair)
        for pair in range(width // PANEL // 2)
        for first in range(0, rows, 2 * CHUNK)
    ]
    for start in range(0, width, PANEL):
        block = slice(start, start + PANEL)
        inverse = right_form(
            panel_inverse(
                [work[start + r : start + r + STEP, block] for r in range(0, PANEL, STEP)],
                jobs,
                spread,
            )
        )
        rights = []
        jobs = [
            block_job(inverse, rights, n, start)
            for n in range(start // PANEL + 1, width // PANEL)
        ]
        if jobs:
            jobs.pop(0)()
        jobs += [rows_job(inverse, rights, first, start) for first in range(0, rows, CHUNK)]
    for job in jobs:
        job()
    ones = jnp.ones((3 * PANEL, LANES), jnp.bfloat16)
    keep = lax.broadcasted_iota(jnp.int32, (LANES, LANES), 0) == lax.broadcasted_iota(
        jnp.int32, (LANES, LANES), 1
    )
    sums = nn_dot(jnp.concatenate(thirds(squares[...]), axis=1), ones)
    for first in range(0, rows, LANES):
        here = slice(first, first + LANES)
        diag_ref[:, here] = 1.0 - jnp.sum(jnp.where(keep, sums[here], 0.0), axis=0, keepdims=True)


def slots_kernel(ndev, rows, slots, pivots_ref, target_ref, column_ref):
    blocks, piv = pivots_ref.shape
    me = lax.axis_index("rows")
    before = jnp.where(
        lax.broadcasted_iota(jnp.int32, (piv, piv), 0)
        < lax.broadcasted_iota(jnp.int32, (piv, piv), 1),
        1.0,
        0.0,
    ).astype(jnp.bfloat16)
    device = lax.broadcasted_iota(jnp.int32, (ndev, piv), 0)
    base = jnp.where(device % 2 == me % 2, 0, ndev // 2 * slots) + device // 2 * slots
    targets = []
    columns = []
    for b in range(blocks):
        pivots = pivots_ref[b : b + 1, :]
        low = device * rows
        owned = jnp.where((pivots >= low) & (pivots < low + rows), 1.0, 0.0)
        count = nn_dot(owned.astype(jnp.bfloat16), before)
        slot = jnp.sum(owned * count, axis=0, keepdims=True)
        targets.append(slot + jnp.sum(owned * base.astype(jnp.float32), axis=0, keepdims=True))
        local = pivots - me * rows
        mine = (local >= 0) & (local < rows)
        wanted = mine & (
            lax.broadcasted_iota(jnp.int32, (slots, piv), 0).astype(jnp.float32) == slot
        )
        columns.append(
            jnp.sum(
                jnp.where(wanted, (local + 1).astype(jnp.float32), 0.0), axis=1, keepdims=True
            )
        )
    target_ref[...] = jnp.concatenate(
        targets + [jnp.zeros((STEP - blocks, piv), jnp.float32)], axis=0
    )
    for b in range(blocks):
        column_ref[b * slots : (b + 1) * slots, :] = jnp.broadcast_to(columns[b], (slots, LANES))


def points_kernel(points_ref, out_ref):
    scale = (2.0 / (1.65 * points_ref.shape[0])) ** 0.5
    out_ref[...] = exponent_operands(points_ref[...].T * scale, True, False)[0]


def pick_kernel(points_ref, column_ref, buffer_ref):
    dim, rows = points_ref.shape
    slots = buffer_ref.shape[1]
    place = lax.broadcasted_iota(jnp.int32, (column_ref.shape[0], rows), 1).astype(jnp.float32)
    chosen = jnp.where(place + 1.0 == column_ref[:, :1], 1.0, 0.0).astype(jnp.bfloat16)
    found = nt_dot(chosen, jnp.concatenate(thirds(points_ref[...]), axis=0))
    found = found[:, :dim] + found[:, dim : 2 * dim] + found[:, 2 * dim :]
    picked = jnp.concatenate([found[:slots], found[slots:]], axis=1)
    buffer_ref[...] = jnp.broadcast_to(picked[None], buffer_ref.shape)


VMEM = pl.BlockSpec(memory_space=pltpu.VMEM)


def prepare(points_t, pivots, ndev, slots):
    dim, rows = points_t.shape
    blocks, piv = pivots.shape
    target, column = pl.pallas_call(
        functools.partial(slots_kernel, ndev, rows, slots),
        out_shape=[
            jax.ShapeDtypeStruct((STEP, piv), jnp.float32),
            jax.ShapeDtypeStruct((blocks * slots, LANES), jnp.float32),
        ],
        in_specs=[VMEM],
        out_specs=[VMEM] * 2,
        compiler_params=pltpu.CompilerParams(vmem_limit_bytes=32 * 2**20),
    )(pivots)
    buffer = pl.pallas_call(
        pick_kernel,
        out_shape=jax.ShapeDtypeStruct((ndev // 2, slots, blocks * dim), jnp.float32),
        in_specs=[VMEM] * 2,
        out_specs=VMEM,
        compiler_params=pltpu.CompilerParams(vmem_limit_bytes=32 * 2**20),
    )(points_t, column)
    points = pl.pallas_call(
        points_kernel,
        out_shape=jax.ShapeDtypeStruct((rows, 256), jnp.bfloat16),
        in_specs=[VMEM],
        out_specs=VMEM,
        compiler_params=pltpu.CompilerParams(vmem_limit_bytes=32 * 2**20),
        cost_estimate=pl.CostEstimate(
            flops=20 * rows * dim, bytes_accessed=3 * rows * 256, transcendentals=0
        ),
    )(points_t)
    return points, buffer, target


def factorize(points, near, other, target, width):
    rows = points.shape[0]
    return pl.pallas_call(
        factor_kernel,
        out_shape=[
            jax.ShapeDtypeStruct((rows, width), jnp.bfloat16),
            jax.ShapeDtypeStruct((1, rows), jnp.float32),
        ],
        in_specs=[VMEM] * 4,
        out_specs=[VMEM] * 2,
        scratch_shapes=[
            pltpu.VMEM((width + rows, width), jnp.float32),
            pltpu.VMEM((rows, PANEL), jnp.float32),
            pltpu.VMEM(((STEP + 1) * PANEL, LANES), jnp.float32),
        ],
        compiler_params=pltpu.CompilerParams(vmem_limit_bytes=48 * 2**20),
    )(points, near, other, target)


def body(points_t, pivots):
    ndev = lax.axis_size("rows")
    dim, rows_here = points_t.shape
    blocks, piv = pivots.shape
    slots = -(-(piv // ndev + 2) // STEP) * STEP
    points, buffer, target = prepare(points_t, pivots, ndev, slots)
    cores = [[d for d in range(ndev) if d % 2 == core] for core in range(2)]
    near = lax.all_to_all(buffer, "rows", 0, 0, axis_index_groups=cores, tiled=True)
    near = near.reshape(ndev // 2 * slots, blocks * dim)
    other = lax.ppermute(near, "rows", [(d, d ^ 1) for d in range(ndev)])
    factor, diag = factorize(points, near, other, target, blocks * piv)
    return (factor, diag.reshape(rows_here))


def solution(mesh):
    return jax.shard_map(
        body,
        mesh=mesh,
        in_specs=(P(None, "rows"), P()),
        out_specs=(P("rows", None), P("rows")),
        check_vma=False,
    )
```

```python
import functools

import jax
import jax.numpy as jnp
from jax import lax
from jax.experimental import pallas as pl
from jax.experimental.pallas import tpu as pltpu
from jax.sharding import PartitionSpec as P

PANEL = 128
STEP = 8
LANES = 128
CHUNK = 1024


def halves(x):
    high = x.astype(jnp.bfloat16)
    return high, (x - high.astype(jnp.float32)).astype(jnp.bfloat16)


def thirds(x):
    high = x.astype(jnp.bfloat16)
    mid, low = halves(x - high.astype(jnp.float32))
    return high, mid, low


def nn_dot(left, right):
    return jnp.dot(left, right, preferred_element_type=jnp.float32)


def nt_dot(left, right):
    return lax.dot_general(
        left, right, (((1,), (1,)), ((), ())), preferred_element_type=jnp.float32
    )


def left_form(x):
    high, low = halves(x)
    return jnp.concatenate([high, high, low], axis=1)


def right_form(x):
    high, low = halves(x)
    return jnp.concatenate([high, low, high], axis=1)


def exponent_operands(x, left, right):
    rows = x.shape[0]
    half = [-h for h in thirds(0.5 * jnp.sum(x * x, axis=1, keepdims=True))]
    one = jnp.ones((rows, 3), jnp.bfloat16)
    pad = jnp.zeros((rows, 256 - 3 * x.shape[1] - 6), jnp.bfloat16)
    high, low = halves(x)
    result = []
    if left:
        result.append(jnp.concatenate([high, high, low] + half + [one, pad], axis=1))
    if right:
        result.append(jnp.concatenate([high, low, high, one] + half + [pad], axis=1))
    return result


def lane_spread(x, lane):
    return jnp.broadcast_to(x[:, lane : lane + 1], (STEP, LANES))


class Spreader:
    def __init__(self, ref):
        self.ref = ref
        self.at = 0

    def rows(self, x, first=0):
        base = self.at
        self.at += STEP
        self.ref[base : base + STEP, :] = x
        return {i: self.ref[pl.ds(base + i, STEP, stride=0), :] for i in range(first, STEP)}


def small_factor(e):
    low = {}
    inv = {}
    for k in range(0, STEP, 2):
        a, b, c = e[k, k], e[k + 1, k], e[k + 1, k + 1]
        root = lax.rsqrt(a * c - b * b)
        inv[k] = lax.rsqrt(a)
        inv[k + 1] = (a * inv[k]) * root
        low[k + 1, k] = b * inv[k]
        for i in range(k + 2, STEP):
            low[i, k] = e[i, k] * inv[k]
            low[i, k + 1] = (e[i, k + 1] - low[i, k] * low[k + 1, k]) * inv[k + 1]
        for m in range(k + 2, STEP):
            for i in range(m, STEP):
                e[i, m] = (e[i, m] - low[i, k] * low[m, k]) - low[i, k + 1] * low[m, k + 1]
    return low, inv


def panel_inverse(tiles, jobs, spread):
    lane = lax.broadcasted_iota(jnp.int32, (STEP, LANES), 1)
    sub = lax.broadcasted_iota(jnp.int32, (STEP, LANES), 0)
    tiles = list(tiles)
    jobs = list(jobs)
    result = []
    spreader = Spreader(spread)
    for s in range(len(tiles)):
        first = STEP * s
        inside = (lane >= first) & (lane < first + STEP)
        cols = [lane_spread(tiles[s], first + k) for k in range(STEP)]
        e = {}
        for k in range(STEP):
            for i, row in spreader.rows(cols[k], k).items():
                e[i, k] = row
        low, inv = small_factor(e)
        own = jnp.where(inside, jnp.where(lane - first == sub, 1.0, 0.0), tiles[s])
        upper = []
        own_rows = spreader.rows(own)
        for i in range(STEP):
            acc = own_rows[i]
            for m in range(i):
                acc = acc - low[i, m] * upper[m]
            upper.append(acc * inv[i])
        done = upper[0]
        for i in range(1, STEP):
            done = jnp.where(sub == i, upper[i], done)
        result.append(jnp.where(lane < first + STEP, done, 0.0))
        full = None
        for t in range(s + 1, len(tiles)):
            cols = [lane_spread(tiles[t], first + k) for k in range(STEP)]
            acc = jnp.where(inside, 0.0, tiles[t])
            if t == s + 1:
                mine = []
                for k in range(STEP):
                    col = cols[k]
                    for m in range(k):
                        col = col - low[k, m] * mine[m]
                    mine.append(col * inv[k])
                    acc = acc - mine[k] * upper[k]
            else:
                if full is None:
                    full = [None] * STEP
                    for i in reversed(range(STEP)):
                        back = upper[i]
                        for m in range(i + 1, STEP):
                            back = back - low[m, i] * full[m]
                        full[i] = back * inv[i]
                for k in range(STEP):
                    acc = acc - cols[k] * full[k]
            tiles[t] = acc
        if jobs:
            jobs.pop(0)()
    for job in jobs:
        job()
    return jnp.concatenate(result, axis=0)


def factor_kernel(points_ref, near_ref, other_ref, target_ref, factor_ref, diag_ref, work, squares, spread):
    rows, width = factor_ref.shape
    dim = near_ref.shape[1] // 2
    piv = width // 2
    scale = (2.0 / (1.65 * dim)) ** 0.5

    gathered = jnp.concatenate([near_ref[...], other_ref[...]], axis=0)
    received = jnp.concatenate(thirds(gathered * scale), axis=1)
    target = target_ref[...].T
    place = lax.broadcasted_iota(jnp.int32, (PANEL, received.shape[0]), 1).astype(jnp.float32)
    piv_left = []
    piv_right = []

    def kernel_block(block):
        def job():
            first = block * PANEL
            half, at = divmod(first, piv)
            chosen = jnp.where(place == target[at : at + PANEL, half : half + 1], 1.0, 0.0)
            found = nn_dot(chosen.astype(jnp.bfloat16), received)
            found = found[:, : 2 * dim] + found[:, 2 * dim : 4 * dim] + found[:, 4 * dim :]
            left, right = exponent_operands(found[:, half * dim : (half + 1) * dim], True, True)
            piv_left.append(left)
            piv_right.append(right)
            for n in range(block + 1):
                work[first : first + PANEL, n * PANEL : (n + 1) * PANEL] = jnp.exp(
                    nt_dot(left, piv_right[n])
                )

        return job

    kernel_block(0)()

    def kernel_rows(first, pair):
        def job():
            right = jnp.concatenate(piv_right[2 * pair : 2 * pair + 2], axis=0)
            cols = slice(2 * pair * PANEL, 2 * (pair + 1) * PANEL)
            here = slice(first, first + CHUNK)
            work[width + first : width + first + CHUNK, cols] = jnp.exp(
                nt_dot(points_ref[here, :], right)
            )

        return job

    def block_job(inverse, rights, block, start):
        def job():
            at = slice(block * PANEL, (block + 1) * PANEL)
            new = nt_dot(left_form(work[at, start : start + PANEL]), inverse)
            rights.append(right_form(new))
            left = left_form(new)
            for n, right in enumerate(rights):
                to = slice(start + PANEL * (n + 1), start + PANEL * (n + 2))
                work[at, to] = work[at, to] - nt_dot(left, right)

        return job

    def rows_job(inverse, rights, first, start):
        def job():
            at = slice(width + first, width + first + CHUNK)
            new = nt_dot(left_form(work[at, start : start + PANEL]), inverse)
            here = slice(first, first + CHUNK)
            factor_ref[here, start : start + PANEL] = new.astype(jnp.bfloat16)
            squares[here, :] = new * new if start == 0 else squares[here, :] + new * new
            if rights:
                work[at, start + PANEL :] = work[at, start + PANEL :] - nt_dot(
                    left_form(new), jnp.concatenate(rights, axis=0)
                )

        return job

    jobs = [kernel_block(block) for block in range(1, width // PANEL)]
    jobs += [
        kernel_rows(first, pair)
        for pair in range(width // PANEL // 2)
        for first in range(0, rows, CHUNK)
    ]
    for start in range(0, width, PANEL):
        block = slice(start, start + PANEL)
        inverse = right_form(
            panel_inverse(
                [work[start + r : start + r + STEP, block] for r in range(0, PANEL, STEP)],
                jobs,
                spread,
            )
        )
        rights = []
        jobs = [
            block_job(inverse, rights, n, start)
            for n in range(start // PANEL + 1, width // PANEL)
        ]
        if jobs:
            jobs.pop(0)()
        jobs += [rows_job(inverse, rights, first, start) for first in range(0, rows, CHUNK)]
    for job in jobs:
        job()
    ones = jnp.ones((3 * PANEL, LANES), jnp.bfloat16)
    keep = lax.broadcasted_iota(jnp.int32, (LANES, LANES), 0) == lax.broadcasted_iota(
        jnp.int32, (LANES, LANES), 1
    )
    sums = nn_dot(jnp.concatenate(thirds(squares[...]), axis=1), ones)
    for first in range(0, rows, LANES):
        here = slice(first, first + LANES)
        diag_ref[:, here] = 1.0 - jnp.sum(jnp.where(keep, sums[here], 0.0), axis=0, keepdims=True)


def slots_kernel(ndev, rows, slots, pivots_ref, target_ref, column_ref):
    blocks, piv = pivots_ref.shape
    me = lax.axis_index("rows")
    before = jnp.where(
        lax.broadcasted_iota(jnp.int32, (piv, piv), 0)
        < lax.broadcasted_iota(jnp.int32, (piv, piv), 1),
        1.0,
        0.0,
    ).astype(jnp.bfloat16)
    device = lax.broadcasted_iota(jnp.int32, (ndev, piv), 0)
    base = jnp.where(device % 2 == me % 2, 0, ndev // 2 * slots) + device // 2 * slots
    targets = []
    columns = []
    for b in range(blocks):
        pivots = pivots_ref[b : b + 1, :]
        low = device * rows
        owned = jnp.where((pivots >= low) & (pivots < low + rows), 1.0, 0.0)
        count = nn_dot(owned.astype(jnp.bfloat16), before)
        slot = jnp.sum(owned * count, axis=0, keepdims=True)
        targets.append(slot + jnp.sum(owned * base.astype(jnp.float32), axis=0, keepdims=True))
        local = pivots - me * rows
        mine = (local >= 0) & (local < rows)
        wanted = mine & (
            lax.broadcasted_iota(jnp.int32, (slots, piv), 0).astype(jnp.float32) == slot
        )
        columns.append(
            jnp.sum(
                jnp.where(wanted, (local + 1).astype(jnp.float32), 0.0), axis=1, keepdims=True
            )
        )
    target_ref[...] = jnp.concatenate(
        targets + [jnp.zeros((STEP - blocks, piv), jnp.float32)], axis=0
    )
    for b in range(blocks):
        column_ref[b * slots : (b + 1) * slots, :] = jnp.broadcast_to(columns[b], (slots, LANES))


def points_kernel(points_ref, out_ref):
    scale = (2.0 / (1.65 * points_ref.shape[0])) ** 0.5
    out_ref[...] = exponent_operands(points_ref[...].T * scale, True, False)[0]


def pick_kernel(points_ref, column_ref, buffer_ref):
    dim, rows = points_ref.shape
    slots = buffer_ref.shape[1]
    place = lax.broadcasted_iota(jnp.int32, (column_ref.shape[0], rows), 1).astype(jnp.float32)
    chosen = jnp.where(place + 1.0 == column_ref[:, :1], 1.0, 0.0).astype(jnp.bfloat16)
    found = nt_dot(chosen, jnp.concatenate(thirds(points_ref[...]), axis=0))
    found = found[:, :dim] + found[:, dim : 2 * dim] + found[:, 2 * dim :]
    picked = jnp.concatenate([found[:slots], found[slots:]], axis=1)
    buffer_ref[...] = jnp.broadcast_to(picked[None], buffer_ref.shape)


VMEM = pl.BlockSpec(memory_space=pltpu.VMEM)


def prepare(points_t, pivots, ndev, slots):
    dim, rows = points_t.shape
    blocks, piv = pivots.shape
    target, column = pl.pallas_call(
        functools.partial(slots_kernel, ndev, rows, slots),
        out_shape=[
            jax.ShapeDtypeStruct((STEP, piv), jnp.float32),
            jax.ShapeDtypeStruct((blocks * slots, LANES), jnp.float32),
        ],
        in_specs=[VMEM],
        out_specs=[VMEM] * 2,
        compiler_params=pltpu.CompilerParams(vmem_limit_bytes=32 * 2**20),
    )(pivots)
    buffer = pl.pallas_call(
        pick_kernel,
        out_shape=jax.ShapeDtypeStruct((ndev // 2, slots, blocks * dim), jnp.float32),
        in_specs=[VMEM] * 2,
        out_specs=VMEM,
        compiler_params=pltpu.CompilerParams(vmem_limit_bytes=32 * 2**20),
    )(points_t, column)
    points = pl.pallas_call(
        points_kernel,
        out_shape=jax.ShapeDtypeStruct((rows, 256), jnp.bfloat16),
        in_specs=[VMEM],
        out_specs=VMEM,
        compiler_params=pltpu.CompilerParams(vmem_limit_bytes=32 * 2**20),
        cost_estimate=pl.CostEstimate(
            flops=20 * rows * dim, bytes_accessed=3 * rows * 256, transcendentals=0
        ),
    )(points_t)
    return points, buffer, target


def factorize(points, near, other, target, width):
    rows = points.shape[0]
    return pl.pallas_call(
        factor_kernel,
        out_shape=[
            jax.ShapeDtypeStruct((rows, width), jnp.bfloat16),
            jax.ShapeDtypeStruct((1, rows), jnp.float32),
        ],
        in_specs=[VMEM] * 4,
        out_specs=[VMEM] * 2,
        scratch_shapes=[
            pltpu.VMEM((width + rows, width), jnp.float32),
            pltpu.VMEM((rows, PANEL), jnp.float32),
            pltpu.VMEM(((STEP + 1) * PANEL, LANES), jnp.float32),
        ],
        compiler_params=pltpu.CompilerParams(vmem_limit_bytes=48 * 2**20),
    )(points, near, other, target)


def body(points_t, pivots):
    ndev = lax.axis_size("rows")
    dim, rows_here = points_t.shape
    blocks, piv = pivots.shape
    slots = -(-(piv // ndev + 2) // STEP) * STEP
    points, buffer, target = prepare(points_t, pivots, ndev, slots)
    cores = [[d for d in range(ndev) if d % 2 == core] for core in range(2)]
    near = lax.all_to_all(buffer, "rows", 0, 0, axis_index_groups=cores, tiled=True)
    near = near.reshape(ndev // 2 * slots, blocks * dim)
    other = lax.ppermute(near, "rows", [(d, d ^ 1) for d in range(ndev)])
    factor, diag = factorize(points, near, other, target, blocks * piv)
    return (factor, diag.reshape(rows_here))


def solution(mesh):
    return jax.shard_map(
        body,
        mesh=mesh,
        in_specs=(P(None, "rows"), P()),
        out_specs=(P("rows", None), P("rows")),
        check_vma=False,
    )
```
